32 devices in a mesh: gy: 8 (over z, y), gz: 4 (over x, core).
Axes of the slice: x: 2, y: 2, z: 4, core: 2. Of those that a mesh axis runs over, the one named last changes fastest.
Arguments:
- observed: float32 [2, 256, 64, 512], P(None, 'gy', 'gz'), may hold values from 0.1 to 4
- psf_rows: float32 [2, 31], replicated, may hold values from 0.05 to 1
- psf_columns: float32 [2, 31], replicated, may hold values from 0.05 to 1
- psf_axial: float32 [2, 101], replicated, may hold values from 0.05 to 1
- live_list: int32 [8, 4, 32], P('gy'), may hold values from -1 to 31, as said below
Outputs:
- estimate: float32 [2, 256, 64, 512], P(None, 'gy', 'gz')
The draws below stay inside these ranges and needn't reach their ends.
Inputs may be any that keep to these rules, and one draw needn't show every extreme that they name: Each row live_list[i, j] lists distinct brick numbers of device (i, j) in any order, followed by entries -1; at least 8 entries of every row are brick numbers, and some row names all 32 bricks.
All inputs are finite; a program needn't handle non-finite values.
Results may differ from the reference program's by a relative error of at most 0.0001.
Values sent between devices are 32-bit elements; how exact they have to be, the bound alone decides.
No kernel may reach another device: no remote copies, remote signals or barrier semaphores. Data moves between devices by JAX's collectives and lax.ppermute only.
A program may use at most 128 MiB of HBM per device.

```python
import math
import jax
import jax.numpy as jnp
from jax import lax

C = 2
KL = 31
KZ = 101
ITERS = 2
Y_DEV = 32
Z_DEV = 16
X = 512
BY = 8
BZ = 8
BX = 128
NB = 32
Y = 256
Z = 64
N_GY = 8
N_GZ = 4


def draw_live_list(key, part):
    key = jax.random.fold_in(key, 11)
    devices_all = N_GY * N_GZ
    order_keys = jax.random.split(jax.random.fold_in(key, 1), devices_all)

    def one_order(order_key):
        return jax.random.permutation(order_key, NB)
    orders = jax.vmap(one_order)(order_keys)
    divisors = jax.random.randint(jax.random.fold_in(key, 2), (devices_all,), 1, 5)
    counts = NB // divisors
    fullest = jax.random.randint(jax.random.fold_in(key, 3), (), 0, devices_all)
    counts = jnp.where(jnp.arange(devices_all) == fullest, NB, counts)
    positions = jnp.arange(NB)[None, :]
    listed = jnp.where(positions < counts[:, None], orders, -1)
    return listed.reshape(N_GY, N_GZ, NB).astype(jnp.int32)


def level_of(rng, dims, pieces, smallest, largest):
    def one(axis_at, shards_of):
        steps = jax.random.uniform(jax.random.fold_in(jax.random.fold_in(rng, 6), axis_at), (shards_of,), jnp.float32, smallest / len(pieces), largest / len(pieces))
        return jnp.repeat(jnp.exp(steps), dims[axis_at] // shards_of).reshape((-1,) + (1,) * (len(dims) - axis_at - 1))

    factor_of = one(*pieces[0])
    for cut in pieces[1:]:
        factor_of = factor_of * one(*cut)
    return factor_of


def setup_inputs(seed: int = 0) -> dict:
    seeds = jax.random.split(jax.random.key(seed), 6)
    observed = jnp.clip(jnp.exp(math.log(4.0) - 3.6888794 * jax.random.uniform(seeds[0], (C, Y, Z, X), jnp.float32) ** level_of(seeds[0], (C, Y, Z, X), ((1, 8), (2, 4)), -0.2, 0.2)), 0.1, 4.0)
    psf_rows = jnp.clip(jnp.exp(jax.random.uniform(seeds[1], (C, KL), jnp.float32, math.log(0.05), math.log(1.0))), 0.05, 1.0)
    psf_columns = jnp.clip(jnp.exp(jax.random.uniform(seeds[2], (C, KL), jnp.float32, math.log(0.05), math.log(1.0))), 0.05, 1.0)
    psf_axial = jnp.clip(jnp.exp(jax.random.uniform(seeds[3], (C, KZ), jnp.float32, math.log(0.05), math.log(1.0))), 0.05, 1.0)
    live_list = draw_live_list(jax.random.fold_in(seeds[5], 71), 0)
    return dict(observed=observed, psf_rows=psf_rows, psf_columns=psf_columns, psf_axial=psf_axial, live_list=live_list)


def normalized(kernel):
    return kernel / jnp.sum(kernel, axis=1, keepdims=True)


def correlate(volume, kernel, axis_number):
    radius = kernel.shape[1] // 2
    channels = kernel.shape[0]
    window_shape = [1, 1, 1]
    window_shape[axis_number - 1] = kernel.shape[1]
    filters = kernel.reshape((channels, 1) + tuple(window_shape))
    padding = [(0, 0), (0, 0), (0, 0)]
    padding[axis_number - 1] = (radius, radius)
    result = lax.conv_general_dilated(volume[None], filters, (1, 1, 1), padding,
                                      feature_group_count=channels,
                                      precision=lax.Precision.HIGHEST)
    return result[0]


def blur_volume(volume, rows_kernel, axial_kernel, columns_kernel):
    return correlate(correlate(correlate(volume, rows_kernel, 1), axial_kernel, 2), columns_kernel, 3)


def spread_cells(bricks):
    tiles, depths, blocks = bricks.shape
    widened = jnp.broadcast_to(bricks[:, None, :, None, :, None], (tiles, BY, depths, BZ, blocks, BX))
    return widened.reshape(tiles * BY, depths * BZ, blocks * BX)


def live_cells(live_list):
    numbers = jnp.arange(NB, dtype=jnp.int32)
    hits = jnp.any(live_list[:, :, :, None] == numbers, axis=2)
    hits = hits.reshape(N_GY, N_GZ, Y_DEV // BY, Z_DEV // BZ, X // BX)
    hits = jnp.transpose(hits, (0, 2, 1, 3, 4)).reshape(N_GY * (Y_DEV // BY), N_GZ * (Z_DEV // BZ), X // BX)
    return spread_cells(hits)


def reference(observed, psf_rows, psf_columns, psf_axial, live_list):
    rows_kernel = normalized(psf_rows)
    columns_kernel = normalized(psf_columns)
    axial_kernel = normalized(psf_axial)
    live = live_cells(live_list)[None]
    estimate = observed
    for iteration in range(ITERS):
        blurred = blur_volume(estimate, rows_kernel, axial_kernel, columns_kernel)
        quotient = jnp.where(live, observed / blurred, 1.0)
        correction = blur_volume(quotient, rows_kernel[:, ::-1], axial_kernel[:, ::-1], columns_kernel[:, ::-1])
        estimate = jnp.where(live, estimate * correction, estimate)
    return estimate
```

```python
import jax
import jax.numpy as jnp
from jax import lax
from jax.experimental import pallas as pl
from jax.experimental.pallas import tpu as pltpu
from jax.sharding import Mesh, PartitionSpec as P

ITERS = 2
BY = 8
BZ = 8
LANES = 128
STRIP = 16
F32, BF16 = jnp.float32, jnp.bfloat16
VMEM = pl.BlockSpec(memory_space=pltpu.VMEM)
SMEM = pl.BlockSpec(memory_space=pltpu.SMEM)
PARAMS = pltpu.CompilerParams(vmem_limit_bytes=40 * 1024 * 1024)


def shape(dims, dtype=F32):
    return jax.ShapeDtypeStruct(dims, dtype)


def halves(cells):
    high = cells.astype(BF16)
    return high, (cells - high.astype(F32)).astype(BF16)


def dot(a, b):
    return jnp.dot(a, b, preferred_element_type=F32)


def other(bits, d):
    return tuple(jnp.where((d >> s) & 1, 1 - b, b) for b, s in zip(bits, (2, 1, 0)))


def deal_kernel(me, observed, *outs):
    for d in range(8):
        yl, zh, zl = other((me[0], me[1], me[2]), d)
        start = pl.multiple_of((2 * yl + zl) * LANES, LANES)
        outs[d][...] = observed[zh, :, :, pl.ds(start, LANES)]


def gather_kernel(me, *rest):
    pieces, out = rest[:8], rest[8]
    for d in range(8):
        yl, zh, zl = other((me[0], me[1], me[2]), d)
        start = pl.multiple_of((2 * yl + zl) * LANES, LANES)
        out[zh, :, :, pl.ds(start, LANES)] = pieces[d][...]


def pack_strips(me, cells, to_pair, to_next):
    groups = LANES // STRIP
    lane_group = lax.broadcasted_iota(jnp.int32, (cells.shape[1], LANES), 1) // STRIP
    left_first = me[2] == 1
    for out, edge in (
        (to_pair, jnp.where(left_first, 0, LANES - STRIP)),
        (to_next, jnp.where(left_first, LANES - STRIP, 0)),
    ):
        def one(y, _):
            total = jnp.zeros((cells.shape[1], LANES), F32)
            for j in range(groups):
                shift = lax.rem(STRIP * j - edge + LANES, LANES)
                total = jnp.where(lane_group == j, pltpu.roll(cells[groups * j + y], shift, 1), total)
            out[y] = total
            return 0

        lax.fori_loop(0, groups, one, 0)


def join_kernel(me, *rest):
    pieces, cells, to_pair, to_next = rest[:8], rest[8], rest[9], rest[10]
    bits = (me[0], me[1], me[2])
    rows, depth = pieces[0].shape[:2]
    for d in range(8):
        yl, zh, zl = other(bits, d)
        y0 = pl.multiple_of(yl * rows, rows)
        z0 = pl.multiple_of((2 * zh + zl) * depth, depth)
        cells[pl.ds(y0, rows), pl.ds(z0, depth), :] = pieces[d][...]
    pack_strips(me, cells, to_pair, to_next)


def weights_kernel(me, rows, columns, axial, *outs):
    channel = me[1]
    nx, nz = LANES, outs[0].shape[0] // 4
    radius, reach = columns.shape[1] // 2, axial.shape[1] // 2

    def toeplitz(taps, offsets):
        def one(k, total):
            return jnp.where(offsets == k, taps[channel, k], total)

        return lax.fori_loop(0, taps.shape[1], one, jnp.zeros(offsets.shape, F32))

    for flip in (False, True):
        wz, wx, wh_edge, wh_inner, wy = outs[5 * flip : 5 * flip + 5]

        def offsets(source, target, half):
            return (target - source if flip else source - target) + half

        def iota(dims, axis):
            return lax.broadcasted_iota(jnp.int32, dims, axis)

        dims = (nz, 2 * nz)
        high, low = halves(toeplitz(axial, offsets(iota(dims, 1) % nz, iota(dims, 0), reach)))
        zero = jnp.zeros(dims, BF16)
        wz[...] = jnp.concatenate(
            [
                jnp.concatenate([high, zero], 1),
                jnp.concatenate([low, zero], 1),
                jnp.concatenate([zero, high], 1),
                jnp.concatenate([zero, low], 1),
            ],
            0,
        )
        dims = (nx, nx)
        high, low = halves(toeplitz(columns, offsets(iota(dims, 0), iota(dims, 1), radius)))
        both = jnp.concatenate([high, low], 1)
        wx[...] = jnp.concatenate([both, both], 0)
        dims = (STRIP, nx)
        wh_edge[...] = jnp.zeros(wh_edge.shape, BF16)
        wh_inner[...] = jnp.zeros(wh_inner.shape, BF16)
        for k, first in ((0, me[2] == 0), (1, me[2] == 1)):
            source = iota(dims, 0) + jnp.where(first, nx, -STRIP)
            both = jnp.concatenate(halves(toeplitz(columns, offsets(source, iota(dims, 1), radius))), 1)
            for j in range(nx // STRIP):
                ref, at = place(j, wh_edge, wh_inner)
                ref[at, k * nx + STRIP * j : k * nx + STRIP * (j + 1), :] = both
        for i in range(rows.shape[1]):
            k = rows.shape[1] - 1 - i if flip else i
            wy[i] = jnp.full((8, LANES), rows[channel, k], F32)


def place(j, edge, inner):
    return (edge, j) if j < 2 else (inner, j - 2) if j < 6 else (edge, j - 4)


def blur_z(weights, slabs):
    depth = slabs[0].shape[0]
    parts = [jnp.concatenate(halves(slab), 0) for slab in slabs]
    stacked = jnp.concatenate(
        [jnp.concatenate(parts[:2], 0), jnp.concatenate(parts[2:], 0)], 1
    )
    out = dot(weights, stacked)
    return [
        out[2 * a * depth : (2 * a + 1) * depth, b * LANES : (b + 1) * LANES]
        + out[(2 * a + 1) * depth : (2 * a + 2) * depth, b * LANES : (b + 1) * LANES]
        for b in range(2)
        for a in range(2)
    ]


def own_kernel(cells, wz, wx, edge, inner):
    rows, depth = cells.shape[:2]

    def one(g, _):
        slabs = blur_z(wz[...], [cells[4 * g + i] for i in range(4)])
        out = dot(jnp.concatenate(halves(jnp.concatenate(slabs, 0)), 1), wx[...])
        out = (out[:, :LANES] + out[:, LANES:]).reshape(4, depth, LANES)

        @pl.when(g < rows // 16)
        def _():
            edge[pl.ds(4 * g, 4)] = out

        @pl.when(g >= 3 * rows // 16)
        def _():
            edge[pl.ds(4 * g - rows // 2, 4)] = out

        @pl.when((g >= rows // 16) & (g < 3 * rows // 16))
        def _():
            inner[pl.ds(4 * g - rows // 4, 4)] = out

        return 0

    lax.fori_loop(0, rows // 4, one, 0)


def strip_terms(strips, weights):
    out = dot(strips, weights)
    out = out[:, :LANES] + out[:, LANES:]
    half = out.shape[0] // 2
    return out[:half] + out[half:]


def edge_kernel(me, own_edge, pair, after, wz, wh, edge, strips, send_a, send_b):
    rows, depth = own_edge.shape[0], own_edge.shape[1]
    for g in range(pair.shape[0] // 4):
        a = blur_z(wz[...], [pair[4 * g + i] for i in range(4)])
        b = blur_z(wz[...], [after[4 * g + i] for i in range(4)])
        high_a, low_a = halves(jnp.concatenate(a, 0))
        high_b, low_b = halves(jnp.concatenate(b, 0))
        at = 4 * depth * g
        half = strips.shape[0] // 2
        strips[at : at + 4 * depth, :] = jnp.concatenate([high_a, high_b], 1)
        strips[half + at : half + at + 4 * depth, :] = jnp.concatenate([low_a, low_b], 1)
    for j in range(4):
        add = strip_terms(strips[...], wh[j]).reshape(8, depth, LANES)
        edge[8 * j : 8 * j + 8] = own_edge[8 * j : 8 * j + 8] + add
    count = send_a.shape[0]
    even = me[3] == 0

    @pl.when(even)
    def _():
        send_a[...] = edge[rows - count :]
        send_b[...] = edge[:count]

    @pl.when(jnp.logical_not(even))
    def _():
        send_a[...] = edge[:count]
        send_b[...] = edge[rows - count :]


def inner_kernel(own_inner, edge, strips, wh, wy, out, inner):
    rows, depth = out.shape[:2]
    for j in range(4):
        add = strip_terms(strips[...], wh[j]).reshape(8, depth, LANES)
        inner[8 * j : 8 * j + 8] = own_inner[8 * j : 8 * j + 8] + add
    radius = wy.shape[0] // 2
    quarter = rows // 4
    chunk = 16

    def source(y):
        if y < quarter:
            return edge, y
        if y < 3 * quarter:
            return inner, y - quarter
        return edge, y - 2 * quarter

    def one(t, _):
        z = pl.ds(pl.multiple_of(8 * t, 8), 8)
        taps = [wy[i] for i in range(wy.shape[0])]
        for first in range(0, rows, chunk):
            sums = [None] * chunk
            for y in range(max(0, first - radius), min(rows, first + chunk + radius)):
                ref, at = source(y)
                cell = ref[at, z, :]
                for o in range(chunk):
                    i = y - (first + o) + radius
                    if 0 <= i < len(taps):
                        term = taps[i] * cell
                        sums[o] = term if sums[o] is None else sums[o] + term
            for o in range(chunk):
                out[first + o, z, :] = sums[o]
        return 0

    lax.fori_loop(0, depth // 8, one, 0)


def add_halo(me, part, recv_a, recv_b, wy, halo, blurred):
    rows, depth = part.shape[:2]
    radius = wy.shape[0] // 2
    even = me[3] == 0
    halo[jnp.where(even, 1, 0)] = recv_a[...]
    halo[jnp.where(even, 0, 1)] = recv_b[...]

    def one(t, _):
        z = pl.ds(pl.multiple_of(8 * t, 8), 8)
        taps = [wy[i] for i in range(wy.shape[0])]
        for side in range(2):
            sums = {}
            for h in range(radius):
                y = h - radius if side == 0 else rows + h
                cell = halo[side, h, z, :]
                for o in range(radius) if side == 0 else range(rows - radius, rows):
                    i = y - o + radius
                    if 0 <= i < len(taps):
                        term = taps[i] * cell
                        sums[o] = sums[o] + term if o in sums else term
            for o in sums:
                blurred[o, z, :] = part[o, z, :] + sums[o]
        return 0

    lax.fori_loop(0, depth // 8, one, 0)


def each_row(rows, radius, part, blurred, do):
    def one(y, _):
        do(y, part[y])
        return 0

    def edge(y, _):
        do(y, blurred[y])
        return 0

    lax.fori_loop(0, radius, edge, 0)
    lax.fori_loop(radius, rows - radius, one, 0)
    lax.fori_loop(rows - radius, rows, edge, 0)


def quotient_kernel(me, part, recv_a, recv_b, wy, observed, live, out, to_pair, to_next, halo, blurred):
    add_halo(me, part, recv_a, recv_b, wy, halo, blurred)
    rows = part.shape[0]

    def do(y, value):
        out[y] = jnp.where(live[y // BY] != 0, observed[y] / value, 1.0)

    each_row(rows, wy.shape[0] // 2, part, blurred, do)
    pack_strips(me, out, to_pair, to_next)


def correct(me, part, recv_a, recv_b, wy, estimate, live, out, halo, blurred):
    add_halo(me, part, recv_a, recv_b, wy, halo, blurred)

    def do(y, value):
        out[y] = jnp.where(live[y // BY] != 0, estimate[y] * value, estimate[y])

    each_row(part.shape[0], wy.shape[0] // 2, part, blurred, do)


def estimate_kernel(me, part, recv_a, recv_b, wy, estimate, live, out, to_pair, to_next, halo, blurred):
    correct(me, part, recv_a, recv_b, wy, estimate, live, out, halo, blurred)
    pack_strips(me, out, to_pair, to_next)


def last_kernel(me, part, recv_a, recv_b, wy, estimate, live, *rest):
    pieces, out, halo, blurred = rest[:8], rest[8], rest[9], rest[10]
    correct(me, part, recv_a, recv_b, wy, estimate, live, out, halo, blurred)
    rows, depth = pieces[0].shape[:2]
    for d in range(8):
        yl, zh, zl = other((me[0], me[1], me[2]), d)
        y0 = pl.multiple_of(yl * rows, rows)
        z0 = pl.multiple_of((2 * zh + zl) * depth, depth)
        pieces[d][...] = out[pl.ds(y0, rows), pl.ds(z0, depth), :]


def call(kernel, out, ins, scratch=(), us=1, name=None):
    many = isinstance(out, (tuple, list))
    return pl.pallas_call(
        kernel,
        out_shape=out,
        in_specs=ins,
        out_specs=[VMEM] * len(out) if many else VMEM,
        scratch_shapes=list(scratch),
        compiler_params=PARAMS,
        cost_estimate=pl.CostEstimate(flops=0, bytes_accessed=int(us * 3.0e6), transcendentals=0),
        name=name,
    )


def per_device(observed, psf_rows, psf_columns, psf_axial, live_list):
    yh = lax.axis_index("yh")
    yl, zh, zl = lax.axis_index("yl"), lax.axis_index("zh"), lax.axis_index("zl")
    me = jnp.stack([yl, zh, zl, yh % 2]).astype(jnp.int32)
    channels, rows, depth, columns = observed.shape
    ny, nz = 2 * rows, 4 * depth
    radius = psf_rows.shape[1] // 2
    group = ("yl", "zh", "zl")

    def trade(pieces):
        return [pieces[0]] + [
            lax.ppermute(pieces[d], group, [(i, i ^ d) for i in range(8)]) for d in range(1, 8)
        ]

    piece = shape((rows, depth, LANES))
    dealt = call(deal_kernel, [piece] * 8, [SMEM, VMEM], us=3, name="deal")(me, observed)
    pieces = trade(dealt)

    def normalized(kernel):
        return kernel / jnp.sum(kernel, axis=1, keepdims=True)

    wide = [
        shape((4 * nz, 4 * nz), BF16),
        shape((2 * LANES, 2 * LANES), BF16),
        shape((4, 2 * LANES, 2 * LANES), BF16),
        shape((4, 2 * LANES, 2 * LANES), BF16),
        shape((psf_rows.shape[1], 8, LANES)),
    ]
    weights = call(weights_kernel, wide * 2, [SMEM] * 4, us=4, name="weights")(
        me, normalized(psf_rows), normalized(psf_columns), normalized(psf_axial)
    )

    listed = live_list[0]
    theirs = lax.ppermute(listed, "yl", [(0, 1), (1, 0)])

    def bricks(lists):
        numbers = jnp.arange(lists.shape[1], dtype=jnp.int32)
        hits = jnp.any(lists[:, :, None] == numbers, axis=1)
        hits = hits.reshape(lists.shape[0], rows // BY, depth // BZ, columns // LANES)
        hits = lax.dynamic_index_in_dim(hits, 2 * yl + zl, 3, False)
        return jnp.transpose(hits, (1, 0, 2)).reshape(rows // BY, -1)

    mine, yours = bricks(listed), bricks(theirs)
    both = jnp.where(yl == 0, jnp.concatenate([mine, yours]), jnp.concatenate([yours, mine]))
    live = jnp.broadcast_to(
        jnp.repeat(both, BZ, 1)[:, :, None].astype(F32), (ny // BY, nz, LANES)
    )

    whole = shape((ny, nz, LANES))
    half = shape((ny // 2, nz, LANES))
    strip = shape((LANES // STRIP, nz, LANES))
    halo = shape((radius, nz, LANES))
    taken, to_pair, to_next = call(
        join_kernel, [whole, strip, strip], [SMEM] + [VMEM] * 8, us=4, name="join"
    )(me, *pieces)

    high = lax.axis_size("yh")
    evens = [p for i in range(0, high - 1, 2) for p in ((i, i + 1), (i + 1, i))]
    odds = [p for i in range(1, high - 1, 2) for p in ((i, i + 1), (i + 1, i))]

    def blur(cells, to_pair, to_next, w):
        wz, wx, wh_edge, wh_inner, wy = w
        after = lax.ppermute(to_next, ("yl", "zl"), [(1, 2), (2, 1)])
        pair = lax.ppermute(to_pair, "zl", [(0, 1), (1, 0)])
        own_edge, own_inner = call(own_kernel, [half, half], [VMEM] * 3, us=6, name="own")(cells, wz, wx)
        edge, strips, send_a, send_b = call(
            edge_kernel,
            [half, shape((2 * strip.shape[0] * nz, 2 * LANES), BF16), halo, halo],
            [SMEM] + [VMEM] * 5,
            us=2, name="edge",
        )(me, own_edge, pair, after, wz, wh_edge)
        recv_a = lax.ppermute(send_a, "yh", evens)
        recv_b = lax.ppermute(send_b, "yh", odds)
        part = call(
            inner_kernel, whole, [VMEM] * 5,
            [pltpu.VMEM(half.shape, F32)], us=5, name="inner",
        )(own_inner, edge, strips, wh_inner, wy)
        return part, recv_a, recv_b, wy

    scratch = [pltpu.VMEM((2,) + halo.shape, F32), pltpu.VMEM(whole.shape, F32)]
    estimate = taken
    for iteration in range(ITERS):
        found = blur(estimate, to_pair, to_next, weights[:5])
        quotient, to_pair, to_next = call(
            quotient_kernel, [whole, strip, strip], [SMEM] + [VMEM] * 6, scratch, us=4, name="quotient"
        )(me, *found, taken, live)
        found = blur(quotient, to_pair, to_next, weights[5:])
        if iteration + 1 < ITERS:
            estimate, to_pair, to_next = call(
                estimate_kernel, [whole, strip, strip], [SMEM] + [VMEM] * 6, scratch, us=4, name="estimate"
            )(me, *found, estimate, live)
    pieces = call(
        last_kernel, [piece] * 8, [SMEM] + [VMEM] * 6,
        [pltpu.VMEM(whole.shape, F32)] + scratch, us=2, name="last",
    )(me, *found, estimate, live)
    return call(gather_kernel, shape(observed.shape), [SMEM] + [VMEM] * 8, us=3, name="gather")(
        me, *trade(pieces)
    )


def solution(mesh):
    fine = Mesh(
        mesh.devices.reshape(mesh.devices.shape[0] // 2, 2, 2, mesh.devices.shape[1] // 2),
        ("yh", "yl", "zh", "zl"),
    )
    spread = P(None, ("yh", "yl"), ("zh", "zl"), None)
    placed = (spread, P(), P(), P(), P(("yh", "yl"), None, None))
    return jax.shard_map(per_device, mesh=fine, in_specs=placed, out_specs=spread, check_vma=False)
```

```python
import jax
import jax.numpy as jnp
from jax import lax
from jax.experimental import pallas as pl
from jax.experimental.pallas import tpu as pltpu
from jax.sharding import Mesh, PartitionSpec as P

ITERS = 2
BY = 8
BZ = 8
LANES = 128
STRIP = 16
F32, BF16 = jnp.float32, jnp.bfloat16
VMEM = pl.BlockSpec(memory_space=pltpu.VMEM)
SMEM = pl.BlockSpec(memory_space=pltpu.SMEM)
PARAMS = pltpu.CompilerParams(vmem_limit_bytes=16 * 1024 * 1024)


def shape(dims, dtype=F32):
    return jax.ShapeDtypeStruct(dims, dtype)


def halves(cells):
    high = cells.astype(BF16)
    return high, (cells - high.astype(F32)).astype(BF16)


def dot(a, b):
    return jnp.dot(a, b, preferred_element_type=F32)


def other(bits, d):
    return tuple(jnp.where((d >> s) & 1, 1 - b, b) for b, s in zip(bits, (2, 1, 0)))


def deal_kernel(me, observed, *outs):
    for d in range(8):
        yl, zh, zl = other((me[0], me[1], me[2]), d)
        start = pl.multiple_of((2 * yl + zl) * LANES, LANES)
        outs[d][...] = observed[zh, :, :, pl.ds(start, LANES)]


def gather_kernel(me, *rest):
    pieces, out = rest[:8], rest[8]
    for d in range(8):
        yl, zh, zl = other((me[0], me[1], me[2]), d)
        start = pl.multiple_of((2 * yl + zl) * LANES, LANES)
        out[zh, :, :, pl.ds(start, LANES)] = pieces[d][...]


def pack_tile(me, z, cells, to_pair, to_next):
    groups = LANES // STRIP
    lane_group = lax.broadcasted_iota(jnp.int32, (8, LANES), 1) // STRIP
    left_first = jnp.full((8, LANES), me[2], jnp.int32) == 1
    for y in range(groups):
        left = right = None
        for j in range(groups):
            cell = cells[groups * j + y]
            cell = pltpu.roll(cell, STRIP * j, 1) if j else cell
            left = cell if left is None else jnp.where(lane_group == j, cell, left)
            right = cell if right is None else jnp.where(lane_group == j - 1, cell, right)
        to_pair[y, z, :] = jnp.where(left_first, left, right)
        to_next[y, z, :] = jnp.where(left_first, right, left)


def tiles(depth, body):
    def one(t, _):
        body(pl.ds(pl.multiple_of(8 * t, 8), 8))
        return 0

    lax.fori_loop(0, depth // 8, one, 0)


def join_kernel(me, *rest):
    pieces, cells, to_pair, to_next = rest[:8], rest[8], rest[9], rest[10]
    bits = (me[0], me[1], me[2])
    rows, depth = pieces[0].shape[:2]
    for d in range(8):
        yl, zh, zl = other(bits, d)
        y0 = pl.multiple_of(yl * rows, rows)
        z0 = pl.multiple_of((2 * zh + zl) * depth, depth)
        cells[pl.ds(y0, rows), pl.ds(z0, depth), :] = pieces[d][...]

    def tile(z):
        pack_tile(me, z, [cells[y, z, :] for y in range(2 * rows)], to_pair, to_next)

    tiles(4 * depth, tile)


def weights_kernel(me, rows, columns, axial, *outs):
    channel = me[1]
    nx, nz = LANES, outs[0].shape[0] // 4
    radius, reach = columns.shape[1] // 2, axial.shape[1] // 2

    def toeplitz(taps, offsets):
        def one(k, total):
            return jnp.where(offsets == k, taps[channel, k], total)

        return lax.fori_loop(0, taps.shape[1], one, jnp.zeros(offsets.shape, F32))

    for flip in (False, True):
        wz, wx, wh_edge, wh_inner, wy = outs[5 * flip : 5 * flip + 5]

        def offsets(source, target, half):
            return (target - source if flip else source - target) + half

        def iota(dims, axis):
            return lax.broadcasted_iota(jnp.int32, dims, axis)

        dims = (nz, 2 * nz)
        high, low = halves(toeplitz(axial, offsets(iota(dims, 1) % nz, iota(dims, 0), reach)))
        zero = jnp.zeros(dims, BF16)
        wz[...] = jnp.concatenate(
            [
                jnp.concatenate([high, zero], 1),
                jnp.concatenate([low, zero], 1),
                jnp.concatenate([zero, high], 1),
                jnp.concatenate([zero, low], 1),
            ],
            0,
        )
        dims = (nx, nx)
        high, low = halves(toeplitz(columns, offsets(iota(dims, 0), iota(dims, 1), radius)))
        both = jnp.concatenate([high, low], 1)
        wx[...] = jnp.concatenate([both, both], 0)
        dims = (STRIP, nx)
        wh_edge[...] = jnp.zeros(wh_edge.shape, BF16)
        wh_inner[...] = jnp.zeros(wh_inner.shape, BF16)
        for k, first in ((0, me[2] == 0), (1, me[2] == 1)):
            source = iota(dims, 0) + jnp.where(first, nx, -STRIP)
            both = jnp.concatenate(halves(toeplitz(columns, offsets(source, iota(dims, 1), radius))), 1)
            groups = nx // STRIP
            for j in range(groups):
                ref, at = place(j, wh_edge, wh_inner)
                group = jnp.where(first, j, (j + groups - 1) % groups)
                ref[at, pl.ds(pl.multiple_of(k * nx + STRIP * group, STRIP), STRIP), :] = both
        for i in range(rows.shape[1]):
            k = rows.shape[1] - 1 - i if flip else i
            wy[i] = jnp.full((8, LANES), rows[channel, k], F32)


def place(j, edge, inner):
    return (edge, j) if j < 2 else (inner, j - 2) if j < 6 else (edge, j - 4)


def blur_z(weights, slabs):
    depth = slabs[0].shape[0]
    parts = [jnp.concatenate(halves(slab), 0) for slab in slabs]
    stacked = jnp.concatenate(
        [jnp.concatenate(parts[:2], 0), jnp.concatenate(parts[2:], 0)], 1
    )
    out = dot(weights, stacked)
    return [
        out[2 * a * depth : (2 * a + 1) * depth, b * LANES : (b + 1) * LANES]
        + out[(2 * a + 1) * depth : (2 * a + 2) * depth, b * LANES : (b + 1) * LANES]
        for b in range(2)
        for a in range(2)
    ]


def own_kernel(cells, wz, wx, edge, inner):
    rows, depth = cells.shape[:2]
    quarter = rows // 4
    for first, out, at in ((0, edge, 0), (3 * quarter, edge, quarter), (quarter, inner, 0), (2 * quarter, inner, quarter)):
        slabs = []
        for g in range(quarter // 4):
            slabs += blur_z(wz[...], [cells[first + 4 * g + i] for i in range(4)])
        both = dot(jnp.concatenate(halves(jnp.concatenate(slabs, 0)), 1), wx[...])
        out[at : at + quarter] = (both[:, :LANES] + both[:, LANES:]).reshape(quarter, depth, LANES)


def strip_terms(strips, weights):
    out = dot(strips, weights)
    out = out[:, :LANES] + out[:, LANES:]
    half = out.shape[0] // 2
    return out[:half] + out[half:]


def edge_kernel(me, own_edge, pair, after, wz, wh, edge, strips, send_a, send_b):
    rows, depth = own_edge.shape[0], own_edge.shape[1]
    for g in range(pair.shape[0] // 4):
        a = blur_z(wz[...], [pair[4 * g + i] for i in range(4)])
        b = blur_z(wz[...], [after[4 * g + i] for i in range(4)])
        high_a, low_a = halves(jnp.concatenate(a, 0))
        high_b, low_b = halves(jnp.concatenate(b, 0))
        at = 4 * depth * g
        half = strips.shape[0] // 2
        strips[at : at + 4 * depth, :] = jnp.concatenate([high_a, high_b], 1)
        strips[half + at : half + at + 4 * depth, :] = jnp.concatenate([low_a, low_b], 1)
    for j in range(4):
        add = strip_terms(strips[...], wh[j]).reshape(8, depth, LANES)
        edge[8 * j : 8 * j + 8] = own_edge[8 * j : 8 * j + 8] + add
    count = send_a.shape[0]
    even = me[3] == 0

    @pl.when(even)
    def _():
        send_a[...] = edge[rows - count :]
        send_b[...] = edge[:count]

    @pl.when(jnp.logical_not(even))
    def _():
        send_a[...] = edge[:count]
        send_b[...] = edge[rows - count :]


def inner_kernel(own_inner, edge, strips, wh, wy, out, inner):
    rows, depth = out.shape[:2]
    for j in range(4):
        add = strip_terms(strips[...], wh[j]).reshape(8, depth, LANES)
        inner[8 * j : 8 * j + 8] = own_inner[8 * j : 8 * j + 8] + add
    radius = wy.shape[0] // 2
    quarter = rows // 4
    chunk = 16

    def source(y):
        if y < quarter:
            return edge, y
        if y < 3 * quarter:
            return inner, y - quarter
        return edge, y - 2 * quarter

    def one(t, _):
        z = pl.ds(pl.multiple_of(8 * t, 8), 8)
        taps = [wy[i] for i in range(wy.shape[0])]
        for first in range(0, rows, chunk):
            sums = [None] * chunk
            for y in range(max(0, first - radius), min(rows, first + chunk + radius)):
                ref, at = source(y)
                cell = ref[at, z, :]
                for o in range(chunk):
                    i = y - (first + o) + radius
                    if 0 <= i < len(taps):
                        term = taps[i] * cell
                        sums[o] = term if sums[o] is None else sums[o] + term
            for o in range(chunk):
                out[first + o, z, :] = sums[o]
        return 0

    lax.fori_loop(0, depth // 8, one, 0)


def with_halo(me, part, recv_a, recv_b, wy, halo, body):
    rows, depth = part.shape[:2]
    radius = wy.shape[0] // 2
    even = me[3] == 0
    halo[jnp.where(even, 1, 0)] = recv_a[...]
    halo[jnp.where(even, 0, 1)] = recv_b[...]

    def tile(z):
        taps = [wy[i] for i in range(wy.shape[0])]
        sums = [part[y, z, :] for y in range(rows)]
        for side in range(2):
            for h in range(radius):
                y = h - radius if side == 0 else rows + h
                cell = halo[side, h, z, :]
                for o in range(radius) if side == 0 else range(rows - radius, rows):
                    i = y - o + radius
                    if 0 <= i < len(taps):
                        sums[o] = sums[o] + taps[i] * cell
        body(z, sums)

    tiles(depth, tile)


def quotient_kernel(me, part, recv_a, recv_b, wy, observed, live, out, to_pair, to_next, halo):
    def body(z, blurred):
        cells = []
        for y in range(len(blurred)):
            cells.append(jnp.where(live[y // BY, z, :] != 0, observed[y, z, :] / blurred[y], 1.0))
            out[y, z, :] = cells[y]
        pack_tile(me, z, cells, to_pair, to_next)

    with_halo(me, part, recv_a, recv_b, wy, halo, body)


def estimate_kernel(me, part, recv_a, recv_b, wy, estimate, live, out, to_pair, to_next, halo):
    def body(z, blurred):
        cells = []
        for y in range(len(blurred)):
            cell = estimate[y, z, :]
            cells.append(jnp.where(live[y // BY, z, :] != 0, cell * blurred[y], cell))
            out[y, z, :] = cells[y]
        pack_tile(me, z, cells, to_pair, to_next)

    with_halo(me, part, recv_a, recv_b, wy, halo, body)


def last_kernel(me, part, recv_a, recv_b, wy, estimate, live, *rest):
    pieces, out, halo = rest[:8], rest[8], rest[9]

    def body(z, blurred):
        for y in range(len(blurred)):
            cell = estimate[y, z, :]
            out[y, z, :] = jnp.where(live[y // BY, z, :] != 0, cell * blurred[y], cell)

    with_halo(me, part, recv_a, recv_b, wy, halo, body)
    rows, depth = pieces[0].shape[:2]
    for d in range(8):
        yl, zh, zl = other((me[0], me[1], me[2]), d)
        y0 = pl.multiple_of(yl * rows, rows)
        z0 = pl.multiple_of((2 * zh + zl) * depth, depth)
        pieces[d][...] = out[pl.ds(y0, rows), pl.ds(z0, depth), :]


def call(kernel, out, ins, scratch=(), us=1, name=None):
    many = isinstance(out, (tuple, list))
    return pl.pallas_call(
        kernel,
        out_shape=out,
        in_specs=ins,
        out_specs=[VMEM] * len(out) if many else VMEM,
        scratch_shapes=list(scratch),
        compiler_params=PARAMS,
        cost_estimate=pl.CostEstimate(flops=0, bytes_accessed=int(us * 3.0e6), transcendentals=0),
        name=name,
    )


def per_device(observed, psf_rows, psf_columns, psf_axial, live_list):
    yh = lax.axis_index("yh")
    yl, zh, zl = lax.axis_index("yl"), lax.axis_index("zh"), lax.axis_index("zl")
    me = jnp.stack([yl, zh, zl, yh % 2]).astype(jnp.int32)
    channels, rows, depth, columns = observed.shape
    ny, nz = 2 * rows, 4 * depth
    radius = psf_rows.shape[1] // 2
    group = ("yl", "zh", "zl")

    def trade(pieces):
        return [pieces[0]] + [
            lax.ppermute(pieces[d], group, [(i, i ^ d) for i in range(8)]) for d in range(1, 8)
        ]

    piece = shape((rows, depth, LANES))
    dealt = call(deal_kernel, [piece] * 8, [SMEM, VMEM], us=3, name="deal")(me, observed)
    pieces = trade(dealt)

    def normalized(kernel):
        return kernel / jnp.sum(kernel, axis=1, keepdims=True)

    wide = [
        shape((4 * nz, 4 * nz), BF16),
        shape((2 * LANES, 2 * LANES), BF16),
        shape((4, 2 * LANES, 2 * LANES), BF16),
        shape((4, 2 * LANES, 2 * LANES), BF16),
        shape((psf_rows.shape[1], 8, LANES)),
    ]
    weights = call(weights_kernel, wide * 2, [SMEM] * 4, us=4, name="weights")(
        me, normalized(psf_rows), normalized(psf_columns), normalized(psf_axial)
    )

    listed = live_list[0]
    theirs = lax.ppermute(listed, "yl", [(0, 1), (1, 0)])

    def bricks(lists):
        numbers = jnp.arange(lists.shape[1], dtype=jnp.int32)
        hits = jnp.any(lists[:, :, None] == numbers, axis=1)
        hits = hits.reshape(lists.shape[0], rows // BY, depth // BZ, columns // LANES)
        hits = lax.dynamic_index_in_dim(hits, 2 * yl + zl, 3, False)
        return jnp.transpose(hits, (1, 0, 2)).reshape(rows // BY, -1)

    mine, yours = bricks(listed), bricks(theirs)
    both = jnp.where(yl == 0, jnp.concatenate([mine, yours]), jnp.concatenate([yours, mine]))
    live = jnp.broadcast_to(
        jnp.repeat(both, BZ, 1)[:, :, None].astype(F32), (ny // BY, nz, LANES)
    )

    whole = shape((ny, nz, LANES))
    half = shape((ny // 2, nz, LANES))
    strip = shape((LANES // STRIP, nz, LANES))
    halo = shape((radius, nz, LANES))
    pieces, weights, live = lax.optimization_barrier((pieces, weights, live))
    taken, to_pair, to_next = call(
        join_kernel, [whole, strip, strip], [SMEM] + [VMEM] * 8, us=4, name="join"
    )(me, *pieces)

    high = lax.axis_size("yh")
    evens = [p for i in range(0, high - 1, 2) for p in ((i, i + 1), (i + 1, i))]
    odds = [p for i in range(1, high - 1, 2) for p in ((i, i + 1), (i + 1, i))]

    def blur(cells, to_pair, to_next, w):
        wz, wx, wh_edge, wh_inner, wy = w
        after = lax.ppermute(to_next, ("yl", "zl"), [(1, 2), (2, 1)])
        pair = lax.ppermute(to_pair, "zl", [(0, 1), (1, 0)])
        own_edge, own_inner = call(own_kernel, [half, half], [VMEM] * 3, us=6, name="own")(cells, wz, wx)
        edge, strips, send_a, send_b = call(
            edge_kernel,
            [half, shape((2 * strip.shape[0] * nz, 2 * LANES), BF16), halo, halo],
            [SMEM] + [VMEM] * 5,
            us=2, name="edge",
        )(me, own_edge, pair, after, wz, wh_edge)
        recv_a = lax.ppermute(send_a, "yh", evens)
        recv_b = lax.ppermute(send_b, "yh", odds)
        part = call(
            inner_kernel, whole, [VMEM] * 5,
            [pltpu.VMEM(half.shape, F32)], us=5, name="inner",
        )(own_inner, edge, strips, wh_inner, wy)
        return part, recv_a, recv_b, wy

    scratch = [pltpu.VMEM((2,) + halo.shape, F32)]
    estimate = taken
    for iteration in range(ITERS):
        found = blur(estimate, to_pair, to_next, weights[:5])
        quotient, to_pair, to_next = call(
            quotient_kernel, [whole, strip, strip], [SMEM] + [VMEM] * 6, scratch, us=4, name="quotient"
        )(me, *found, taken, live)
        found = blur(quotient, to_pair, to_next, weights[5:])
        if iteration + 1 < ITERS:
            estimate, to_pair, to_next = call(
                estimate_kernel, [whole, strip, strip], [SMEM] + [VMEM] * 6, scratch, us=4, name="estimate"
            )(me, *found, estimate, live)
    pieces = call(
        last_kernel, [piece] * 8, [SMEM] + [VMEM] * 6,
        [pltpu.VMEM(whole.shape, F32)] + scratch, us=2, name="last",
    )(me, *found, estimate, live)
    return call(gather_kernel, shape(observed.shape), [SMEM] + [VMEM] * 8, us=3, name="gather")(
        me, *trade(pieces)
    )


def solution(mesh):
    fine = Mesh(
        mesh.devices.reshape(mesh.devices.shape[0] // 2, 2, 2, mesh.devices.shape[1] // 2),
        ("yh", "yl", "zh", "zl"),
    )
    spread = P(None, ("yh", "yl"), ("zh", "zl"), None)
    placed = (spread, P(), P(), P(), P(("yh", "yl"), None, None))
    return jax.shard_map(per_device, mesh=fine, in_specs=placed, out_specs=spread, check_vma=False)
```

```python
import functools

import jax
import jax.numpy as jnp
from jax import lax
from jax.experimental import pallas as pl
from jax.experimental.pallas import tpu as pltpu
from jax.sharding import Mesh, PartitionSpec as P

ITERS = 2
BY = 8
BZ = 8
LANES = 128
STRIP = 16
F32, BF16 = jnp.float32, jnp.bfloat16
VMEM = pl.BlockSpec(memory_space=pltpu.VMEM)
SMEM = pl.BlockSpec(memory_space=pltpu.SMEM)
MIB = 1024 * 1024


def shape(dims, dtype=F32):
    return jax.ShapeDtypeStruct(dims, dtype)


def halves(cells):
    high = cells.astype(BF16)
    return high, (cells - high.astype(F32)).astype(BF16)


def dot(a, b):
    return jnp.dot(a, b, preferred_element_type=F32)


def chip(me, e):
    return tuple(jnp.where((e >> s) & 1, 1 - b, b) for b, s in ((me[0], 1), (me[1], 0)))


def slots(start, size):
    return pl.ds(pl.multiple_of(start * size, size), size)


def deal_kernel(me, observed, kept, sent):
    channels, rows, depth, columns = observed.shape
    lane_group = lax.broadcasted_iota(jnp.int32, (8, LANES), 1) // STRIP
    upper = jnp.full((8, LANES), me[0], jnp.int32) == 1
    for c in range(channels):
        for q in range(columns // LANES):
            cells = observed[c, :, :, q * LANES : (q + 1) * LANES]
            strips = {}
            for part in range(2):
                for y in range(4):
                    for t in range(depth // 8):
                        z = slice(8 * t, 8 * t + 8)
                        total = jnp.zeros((8, LANES), F32)
                        for g in range(4):
                            row = 16 * part + 4 * g + y
                            if (q + 1) * LANES < columns:
                                cell = observed[c, row, z, (q + 1) * LANES : (q + 2) * LANES]
                                total = jnp.where(lane_group == g, pltpu.roll(cell, STRIP * g, 1) if g else cell, total)
                            if q:
                                cell = observed[c, row, z, (q - 1) * LANES : q * LANES]
                                cell = pltpu.roll(cell, STRIP * (g + 5), 1)
                                total = jnp.where(lane_group == g + 4, cell, total)
                        strips[part, y, t] = jnp.where(upper, pltpu.roll(total, LANES // 2, 1), total)

            def put(out):
                out[c, q // 2, :rows] = cells
                for (part, y, t), value in strips.items():
                    out[c, q // 2, rows + 4 * part + y, 8 * t : 8 * t + 8, :] = value

            own = me[2] == (q % 2) ^ (q // 2)

            @pl.when(own)
            def _():
                put(kept)

            @pl.when(jnp.logical_not(own))
            def _():
                put(sent)


def mix_kernel(me, kept, swapped, *outs):
    rows, depth = outs[0].shape[0] - 4, kept.shape[3]
    for part in range(2):
        half = me[0] if part == 0 else 1 - me[0]
        for e in range(4):
            yl, zh = chip(me, e)
            out = outs[4 * part + e]
            for z, cells in ((me[2], kept), (1 - me[2], swapped)):
                out[:rows, slots(z, depth), :] = cells[zh, yl, slots(half, rows)]
                out[rows:, slots(z, depth), :] = cells[zh, yl, pl.ds(2 * rows + 4 * half, 4)]


def join_kernel(me, *rest):
    pieces, cells, pair, after, strips = rest[:4], rest[4], rest[5], rest[6], rest[7]
    rows, depth = pieces[0].shape[0] - 4, pieces[0].shape[1]
    for e in range(4):
        yl, zh = chip(me, e)
        z = slots(zh, depth)
        cells[slots(yl, rows), z, :] = pieces[e][:rows]
        strips[yl, :, z, :] = pieces[e][rows:]
    low = lax.broadcasted_iota(jnp.int32, (8, LANES), 1) < LANES // 2
    right_first = jnp.full((8, LANES), me[4], jnp.int32) == 0

    def tile(z):
        for y in range(4):
            first, second = strips[0, y, z, :], strips[1, y, z, :]
            right = jnp.where(low, first, second)
            left = pltpu.roll(jnp.where(low, second, first), 3 * STRIP, 1)
            pair[y, z, :] = jnp.where(right_first, right, left)
            after[y, z, :] = jnp.where(right_first, left, right)

    tiles(cells.shape[1], tile)


def split_depth_kernel(me, *rest):
    pieces, out = rest[:4], rest[4]
    for e in range(4):
        out[e] = pieces[e][:, slots(1 - me[2], out.shape[2]), :]


def gather_kernel(me, *rest):
    out = rest[10]
    for part in range(2):
        pieces, swapped = rest[5 * part : 5 * part + 4], rest[5 * part + 4]
        rows, depth = swapped.shape[1:3]
        y = slots(me[0] if part == 0 else 1 - me[0], rows)
        for e in range(4):
            yl, zh = chip(me, e)
            side = me[2] ^ yl
            out[zh, y, :, slots(2 * yl + side, LANES)] = pieces[e][:, slots(me[2], depth), :]
            out[zh, y, :, slots(2 * yl + 1 - side, LANES)] = swapped[e]


def pack_tile(me, z, cells, to_pair, to_next):
    groups = LANES // STRIP
    deep = len(cells) // groups
    lane_group = lax.broadcasted_iota(jnp.int32, (8, LANES), 1) // STRIP
    left_first = jnp.full((8, LANES), me[4], jnp.int32) == 1
    for y in range(deep):
        left = right = None
        for j in range(groups):
            cell = cells[deep * j + y]
            cell = pltpu.roll(cell, STRIP * j, 1) if j else cell
            left = cell if left is None else jnp.where(lane_group == j, cell, left)
            right = cell if right is None else jnp.where(lane_group == j - 1, cell, right)
        to_pair[y, z, :] = jnp.where(left_first, left, right)
        to_next[y, z, :] = jnp.where(left_first, right, left)


def tiles(depth, body):
    def one(t, _):
        body(pl.ds(pl.multiple_of(8 * t, 8), 8))
        return 0

    lax.fori_loop(0, depth // 8, one, 0)


def weights_kernel(me, rows, columns, axial, listed, theirs, *outs):
    live = outs[-1]
    tall, deep = live.shape[0] // 2, live.shape[1] // listed.shape[0] // BZ
    wide = listed.shape[1] // tall // deep
    for lists, half in ((listed, me[0]), (theirs, 1 - me[0])):
        for g in range(lists.shape[0]):
            bits = jnp.int32(0)
            for i in range(lists.shape[1]):
                number = lists[g, i]
                bits = bits | jnp.where(number < 0, 0, jnp.left_shift(jnp.int32(1), jnp.maximum(number, 0)))
            for t in range(tall):
                for b in range(deep):
                    number = (t * deep + b) * wide + 2 * me[0] + me[4]
                    z = (g * deep + b) * BZ
                    hit = jnp.right_shift(bits, number) & 1
                    live[half * tall + t, z : z + BZ, :] = jnp.full((BZ, LANES), hit, jnp.int32).astype(F32)
    channel = me[1]
    nx, nz = LANES, outs[0].shape[0] // 4
    radius, reach = columns.shape[1] // 2, axial.shape[1] // 2

    totals = {}
    for taps in (rows, columns, axial):
        total = taps[channel, 0]
        for k in range(1, taps.shape[1]):
            total = total + taps[channel, k]
        totals[id(taps)] = total

    def toeplitz(taps, offsets):
        total = jnp.zeros(offsets.shape, F32)
        for k in range(taps.shape[1]):
            total = jnp.where(offsets == k, taps[channel, k], total)
        return total / totals[id(taps)]

    for flip in (False, True):
        wz, wx, wh, wy = outs[4 * flip : 4 * flip + 4]

        def offsets(source, target, half):
            return (target - source if flip else source - target) + half

        def iota(dims, axis):
            return lax.broadcasted_iota(jnp.int32, dims, axis)

        dims = (nz, 2 * nz)
        high, low = halves(toeplitz(axial, offsets(iota(dims, 1) % nz, iota(dims, 0), reach)))
        zero = jnp.zeros(dims, BF16)
        wz[...] = jnp.concatenate(
            [
                jnp.concatenate([high, zero], 1),
                jnp.concatenate([low, zero], 1),
                jnp.concatenate([zero, high], 1),
                jnp.concatenate([zero, low], 1),
            ],
            0,
        )
        dims = (nx, nx)
        high, low = halves(toeplitz(columns, offsets(iota(dims, 0), iota(dims, 1), radius)))
        both = jnp.concatenate([high, low], 1)
        wx[...] = jnp.concatenate([both, both], 0)
        dims = (STRIP, 2 * nx)
        lanes = iota(dims, 1)
        edge = lanes % (2 * STRIP)
        target = jnp.where(edge < STRIP, nx - STRIP + edge, edge - STRIP)
        groups = nx // STRIP
        for k, first in ((0, me[4] == 0), (1, me[4] == 1)):
            source = iota(dims, 0) + jnp.where(first, nx, -STRIP)
            high, low = halves(toeplitz(columns, offsets(source, target, radius)))
            for g in range(groups):
                here = lanes // (2 * STRIP) == jnp.where(first, g, (g + 1) % groups)
                at = k * nx + STRIP * g
                both = [jnp.where(here, part.astype(F32), 0.0).astype(BF16) for part in (high, low)]
                wh[at : at + STRIP, :] = jnp.concatenate(both, 1)
        for i in range(rows.shape[1]):
            k = rows.shape[1] - 1 - i if flip else i
            wy[i] = jnp.full((8, LANES), rows[channel, k], F32) / totals[id(rows)]


def blur_z(weights, slabs):
    depth = slabs[0].shape[0]
    parts = [jnp.concatenate(halves(slab), 0) for slab in slabs]
    stacked = jnp.concatenate(
        [jnp.concatenate(parts[:2], 0), jnp.concatenate(parts[2:], 0)], 1
    )
    out = dot(weights, stacked)
    return [
        out[2 * a * depth : (2 * a + 1) * depth, b * LANES : (b + 1) * LANES]
        + out[(2 * a + 1) * depth : (2 * a + 2) * depth, b * LANES : (b + 1) * LANES]
        for b in range(2)
        for a in range(2)
    ]


def own_columns(cells, wz, wx, out):
    rows, depth = cells.shape[:2]
    count = 16
    for first in range(0, rows, count):
        slabs = []
        for y in range(first, first + count, 4):
            slabs += blur_z(wz[...], [cells[y + i] for i in range(4)])
        both = dot(jnp.concatenate(halves(jnp.concatenate(slabs, 0)), 1), wx[...])
        out[first : first + count] = (both[:, :LANES] + both[:, LANES:]).reshape(count, depth, LANES)


def near_columns(own, pair, after, wz, wh, out):
    deep, depth = pair.shape[:2]
    a = blur_z(wz[...], [pair[i] for i in range(deep)])
    b = blur_z(wz[...], [after[i] for i in range(deep)])
    high_a, low_a = halves(jnp.concatenate(a, 0))
    high_b, low_b = halves(jnp.concatenate(b, 0))
    strips = jnp.concatenate(
        [jnp.concatenate([high_a, high_b], 1), jnp.concatenate([low_a, low_b], 1)], 0
    )
    both = dot(strips, wh[...])
    count, wide = deep * depth, both.shape[1] // 2
    both = both[:, :wide] + both[:, wide:]
    both = both[:count] + both[count:]
    lane = lax.broadcasted_iota(jnp.int32, (count, LANES), 1)
    near = (lane < STRIP) | (lane >= LANES - STRIP)
    per = LANES // (2 * STRIP)
    for j in range(LANES // STRIP):
        add = both[:, j // per * LANES : (j // per + 1) * LANES]
        add = pltpu.roll(add, (LANES - STRIP - 2 * STRIP * (j % per)) % LANES, 1)
        add = jnp.where(near, add, 0.0).reshape(deep, depth, LANES)
        out[deep * j : deep * (j + 1)] = own[deep * j : deep * (j + 1)] + add


def own_kernel(cells, wz, wx, out):
    own_columns(cells, wz, wx, out)


def outer_kernel(me, own, pair, after, wz, wh, out, send_a, send_b):
    near_columns(own, pair, after, wz, wh, out)
    rows, count = out.shape[0], send_a.shape[0]
    even = me[3] == 0

    @pl.when(even)
    def _():
        send_a[...] = out[rows - count :]
        send_b[...] = out[:count]

    @pl.when(jnp.logical_not(even))
    def _():
        send_a[...] = out[:count]
        send_b[...] = out[rows - count :]


def ratio(observed, blurred, live):
    return jnp.where(live != 0, observed / blurred, 1.0)


def product(estimate, correction, live):
    return jnp.where(live != 0, estimate * correction, estimate)


def inner_blur(me, cells, pair, after, outer, wz, wx, wh, wy, part, inner, body):
    own_columns(cells, wz, wx, inner)
    near_columns(inner, pair, after, wz, wh, inner)
    quarter, depth = outer.shape[0] // 2, outer.shape[1]
    rows = 4 * quarter
    radius = wy.shape[0] // 2

    def source(y):
        if y < quarter:
            return outer, y
        if y < 3 * quarter:
            return inner, y - quarter
        return outer, y - 2 * quarter

    def tile(z):
        taps = [wy[i] for i in range(wy.shape[0])]
        blurred = []
        for first in range(0, rows, quarter):
            sums = [None] * quarter
            for y in range(max(0, first - radius), min(rows, first + quarter + radius)):
                ref, at = source(y)
                cell = ref[at, z, :]
                for o in range(quarter):
                    i = y - (first + o) + radius
                    if 0 <= i < len(taps):
                        term = taps[i] * cell
                        sums[o] = term if sums[o] is None else sums[o] + term
            for o in range(quarter):
                ref, at = source(first + o)
                if ref is outer:
                    part[at, z, :] = sums[o]
                else:
                    blurred.append(sums[o])
        body(z, blurred)

    tiles(depth, tile)


def outer_blur(me, part, recv_a, recv_b, wy, halo, body):
    rows, depth = part.shape[:2]
    radius = wy.shape[0] // 2
    even = me[3] == 0
    halo[jnp.where(even, 1, 0)] = recv_a[...]
    halo[jnp.where(even, 0, 1)] = recv_b[...]

    def tile(z):
        taps = [wy[i] for i in range(wy.shape[0])]
        sums = [part[y, z, :] for y in range(rows)]
        for side in range(2):
            for h in range(radius):
                y = h - radius if side == 0 else rows + h
                cell = halo[side, h, z, :]
                for o in range(radius) if side == 0 else range(rows - radius, rows):
                    i = y - o + radius
                    if 0 <= i < len(taps):
                        sums[o] = sums[o] + taps[i] * cell
        body(z, sums)

    tiles(depth, tile)


def bricks_of(outer, y):
    return y // BY if outer and y < 16 else y // BY + (4 if outer else 2)


def update(me, outer, rule, base, live, out, strips):
    def body(z, blurred):
        cells = []
        for y in range(len(blurred)):
            cells.append(rule(base[y, z, :], blurred[y], live[bricks_of(outer, y), z, :]))
            out[y, z, :] = cells[y]
        if strips:
            pack_tile(me, z, cells, *strips)

    return body


def deal_out(me, cells, pieces):
    rows, depth = pieces[0].shape[:2]
    for e in range(4):
        yl, zh = chip(me, e)
        pieces[e][...] = cells[slots(yl, rows), slots(zh, depth), :]


def inner_kernel(rule, me, cells, pair, after, outer, wz, wx, wh, wy, base, live, part, out, to_pair, to_next, inner):
    body = update(me, False, rule, base, live, out, (to_pair, to_next))
    inner_blur(me, cells, pair, after, outer, wz, wx, wh, wy, part, inner, body)


def last_inner_kernel(me, cells, pair, after, outer, wz, wx, wh, wy, base, live, part, *rest):
    pieces, inner, out = rest[:4], rest[4], rest[5]
    body = update(me, False, product, base, live, out, ())
    inner_blur(me, cells, pair, after, outer, wz, wx, wh, wy, part, inner, body)
    deal_out(me, out, pieces)


def final_kernel(rule, me, part, recv_a, recv_b, wy, base, live, out, to_pair, to_next, halo):
    outer_blur(me, part, recv_a, recv_b, wy, halo, update(me, True, rule, base, live, out, (to_pair, to_next)))


def last_final_kernel(me, part, recv_a, recv_b, wy, base, live, *rest):
    pieces, halo, out = rest[:4], rest[4], rest[5]
    outer_blur(me, part, recv_a, recv_b, wy, halo, update(me, True, product, base, live, out, ()))
    deal_out(me, out, pieces)


def call(kernel, out, ins, scratch=(), us=1, name=None, mib=6):
    many = isinstance(out, (tuple, list))
    return pl.pallas_call(
        kernel,
        out_shape=out,
        in_specs=ins,
        out_specs=[VMEM] * len(out) if many else VMEM,
        scratch_shapes=list(scratch),
        compiler_params=pltpu.CompilerParams(vmem_limit_bytes=mib * MIB),
        cost_estimate=pl.CostEstimate(flops=int(us * 1.0e9), bytes_accessed=0, transcendentals=0),
        name=name,
    )


def per_device(observed, psf_rows, psf_columns, psf_axial, live_list):
    yh = lax.axis_index("yh")
    yl, zh, zl = lax.axis_index("yl"), lax.axis_index("zh"), lax.axis_index("zl")
    side = zl ^ yl
    me = jnp.stack([yl, zh, zl, yh % 2, side]).astype(jnp.int32)
    channels, rows, depth, columns = observed.shape
    ny, nz = 2 * rows, 4 * depth
    radius = psf_rows.shape[1] // 2
    swaps = [(0, 1), (1, 0)]

    def trade(pieces):
        return [pieces[0]] + [
            lax.ppermute(pieces[e], ("yl", "zh"), [(i, i ^ e) for i in range(4)]) for e in range(1, 4)
        ]

    half = shape((ny // 2, nz, LANES))
    strip = shape((ny // 2 // (LANES // STRIP), nz, LANES))
    halo = shape((radius, nz, LANES))
    swapped = shape((4, rows // 2, depth, LANES))
    along = shape((rows // 2, 2 * depth, LANES))

    listed = live_list[0]
    theirs = lax.ppermute(listed, "yl", swaps)
    mine = shape((channels, 2, rows + 8, depth, LANES))
    kept, sent = call(deal_kernel, [mine] * 2, [SMEM, VMEM], us=0, name="deal")(me, observed)
    swapped_in = lax.ppermute(sent, "zl", swaps)
    tall = shape((rows // 2 + 4, 2 * depth, LANES))

    dealt = call(mix_kernel, [tall] * 8, [SMEM] + [VMEM] * 2, us=0, name="mix")(me, kept, swapped_in)
    dealt, theirs = lax.optimization_barrier((dealt, theirs))
    outer_pieces = trade(dealt[:4])
    inner_pieces = trade(dealt[4:])

    wide = [
        shape((4 * nz, 4 * nz), BF16),
        shape((2 * LANES, 2 * LANES), BF16),
        shape((2 * LANES, 4 * LANES), BF16),
        shape((psf_rows.shape[1], 8, LANES)),
    ]
    later, _ = lax.optimization_barrier((me, dealt))
    *weights, live = call(
        weights_kernel, wide * 2 + [shape((ny // BY, nz, LANES))], [SMEM] * 6, us=1, name="weights", mib=8
    )(later, psf_rows, psf_columns, psf_axial, listed, theirs)
    outer_pieces, weights, live = lax.optimization_barrier((outer_pieces, weights, live))

    def take(pieces):
        room = pltpu.VMEM((2,) + strip.shape, F32)
        return call(join_kernel, [half, strip, strip], [SMEM] + [VMEM] * 4, [room], us=0.3, name="join")(me, *pieces)

    high = lax.axis_size("yh")
    evens = [p for i in range(0, high - 1, 2) for p in ((i, i + 1), (i + 1, i))]
    odds = [p for i in range(1, high - 1, 2) for p in ((i, i + 1), (i + 1, i))]

    def exchange(to_pair, to_next):
        after = lax.ppermute(to_next, ("yl", "zl"), [(1, 3), (3, 1)])
        return lax.ppermute(to_pair, "zl", swaps), after

    def send_outer(cells, beside, w, near):
        wz, wx, wh, wy = w
        pair, after = beside
        cells, near = lax.optimization_barrier((cells, near))
        own = call(own_kernel, half, [VMEM] * 3, us=0.3, name="own", mib=8)(cells, wz, wx)
        outer, send_a, send_b = call(
            outer_kernel, [half, halo, halo], [SMEM] + [VMEM] * 5, us=0.3, name="outer", mib=8
        )(me, own, pair, after, wz, wh)
        return outer, lax.ppermute(send_a, "yh", evens), lax.ppermute(send_b, "yh", odds), near

    room, beyond = pltpu.VMEM(half.shape, F32), pltpu.VMEM((2,) + halo.shape, F32)
    taken = [take(outer_pieces), None]
    estimate = [taken[0][0], None]
    cells, strips = list(estimate), [taken[0][1:], None]
    for step in range(2 * ITERS):
        w = weights[:4] if step % 2 == 0 else weights[4:]
        near = exchange(*strips[1]) if step else ()
        beside = exchange(*strips[0]) if step else strips[0]
        outer, recv_a, recv_b, near = send_outer(cells[0], beside, w, near)
        if step == 0:
            inner_pieces, outer = lax.optimization_barrier((inner_pieces, outer))
            taken[1] = take(inner_pieces)
            estimate[1] = cells[1] = taken[1][0]
            near = taken[1][1:]
        base = [taken[0][0], taken[1][0]] if step % 2 == 0 else estimate
        ins = (me, cells[1], *near, outer, *w, base[1], live)
        if step == 2 * ITERS - 1:
            part, *pieces = call(
                last_inner_kernel, [half] + [along] * 4, [SMEM] + [VMEM] * 10, [room, room], us=3, name="last_inner", mib=16
            )(*ins)
            inner_out = trade(pieces)
            outer_out = trade(
                call(last_final_kernel, [along] * 4, [SMEM] + [VMEM] * 6, [beyond, room], us=2, name="last", mib=8)(
                    me, part, recv_a, recv_b, w[3], base[0], live
                )
            )
            continue
        rule = ratio if step % 2 == 0 else product
        part, inner, *inner_strips = call(
            functools.partial(inner_kernel, rule), [half, half, strip, strip], [SMEM] + [VMEM] * 10, [room], us=3,
            name="inner", mib=16,
        )(*ins)
        outer, *outer_strips = call(
            functools.partial(final_kernel, rule), [half, strip, strip], [SMEM] + [VMEM] * 6, [beyond], us=2,
            name="final", mib=8,
        )(me, part, recv_a, recv_b, w[3], base[0], live)
        cells, strips = [outer, inner], [outer_strips, inner_strips]
        if step % 2 == 1:
            estimate = cells

    def back(pieces):
        sent = call(split_depth_kernel, swapped, [SMEM] + [VMEM] * 4, us=1, name="split_back")(me, *pieces)
        return (*pieces, lax.ppermute(sent, "zl", swaps))

    return call(gather_kernel, shape(observed.shape), [SMEM] + [VMEM] * 10, us=2, name="gather", mib=8)(
        me, *back(outer_out), *back(inner_out)
    )


def solution(mesh):
    fine = Mesh(
        mesh.devices.reshape(mesh.devices.shape[0] // 2, 2, 2, mesh.devices.shape[1] // 2),
        ("yh", "yl", "zh", "zl"),
    )
    spread = P(None, ("yh", "yl"), ("zh", "zl"), None)
    placed = (spread, P(), P(), P(), P(("yh", "yl"), None, None))
    return jax.shard_map(per_device, mesh=fine, in_specs=placed, out_specs=spread, check_vma=False)
```

```python
import functools

import jax
import jax.numpy as jnp
from jax import lax
from jax.experimental import pallas as pl
from jax.experimental.pallas import tpu as pltpu
from jax.sharding import Mesh, PartitionSpec as P

ITERS = 2
BY = 8
BZ = 8
LANES = 128
STRIP = 16
F32, BF16 = jnp.float32, jnp.bfloat16
VMEM = pl.BlockSpec(memory_space=pltpu.VMEM)
SMEM = pl.BlockSpec(memory_space=pltpu.SMEM)
MIB = 1024 * 1024


def shape(dims, dtype=F32):
    return jax.ShapeDtypeStruct(dims, dtype)


def halves(cells):
    high = cells.astype(BF16)
    return high, (cells - high.astype(F32)).astype(BF16)


def dot(a, b):
    return jnp.dot(a, b, preferred_element_type=F32)


def chip(me, e):
    return tuple(jnp.where((e >> s) & 1, 1 - b, b) for b, s in ((me[0], 1), (me[1], 0)))


def slots(start, size):
    return pl.ds(pl.multiple_of(start * size, size), size)


def deal_kernel(me, observed, kept, sent):
    channels, rows, depth, columns = observed.shape
    lane_group = lax.broadcasted_iota(jnp.int32, (8, LANES), 1) // STRIP
    upper = jnp.full((8, LANES), me[0], jnp.int32) == 1
    for c in range(channels):
        for q in range(columns // LANES):
            cells = observed[c, :, :, q * LANES : (q + 1) * LANES]
            strips = {}
            for part in range(2):
                for y in range(4):
                    for t in range(depth // 8):
                        z = slice(8 * t, 8 * t + 8)
                        total = jnp.zeros((8, LANES), F32)
                        for g in range(4):
                            row = 16 * part + 4 * g + y
                            if (q + 1) * LANES < columns:
                                cell = observed[c, row, z, (q + 1) * LANES : (q + 2) * LANES]
                                total = jnp.where(lane_group == g, pltpu.roll(cell, STRIP * g, 1) if g else cell, total)
                            if q:
                                cell = observed[c, row, z, (q - 1) * LANES : q * LANES]
                                cell = pltpu.roll(cell, STRIP * (g + 5), 1)
                                total = jnp.where(lane_group == g + 4, cell, total)
                        strips[part, y, t] = jnp.where(upper, pltpu.roll(total, LANES // 2, 1), total)

            def put(out):
                out[c, q // 2, :rows] = cells
                for (part, y, t), value in strips.items():
                    out[c, q // 2, rows + 4 * part + y, 8 * t : 8 * t + 8, :] = value

            own = me[2] == (q % 2) ^ (q // 2)

            @pl.when(own)
            def _():
                put(kept)

            @pl.when(jnp.logical_not(own))
            def _():
                put(sent)


def mix_kernel(me, kept, swapped, *outs):
    rows, depth = outs[0].shape[0] - 4, kept.shape[3]
    for part in range(2):
        half = me[0] if part == 0 else 1 - me[0]
        for e in range(4):
            yl, zh = chip(me, e)
            out = outs[4 * part + e]
            for z, cells in ((me[2], kept), (1 - me[2], swapped)):
                out[:rows, slots(z, depth), :] = cells[zh, yl, slots(half, rows)]
                out[rows:, slots(z, depth), :] = cells[zh, yl, pl.ds(2 * rows + 4 * half, 4)]


def join_kernel(me, *rest):
    pieces, cells, pair, after, strips = rest[:4], rest[4], rest[5], rest[6], rest[7]
    rows, depth = pieces[0].shape[0] - 4, pieces[0].shape[1]
    for e in range(4):
        yl, zh = chip(me, e)
        z = slots(zh, depth)
        cells[slots(yl, rows), z, :] = pieces[e][:rows]
        strips[yl, :, z, :] = pieces[e][rows:]
    low = lax.broadcasted_iota(jnp.int32, (8, LANES), 1) < LANES // 2
    right_first = jnp.full((8, LANES), me[4], jnp.int32) == 0

    def tile(z):
        for y in range(4):
            first, second = strips[0, y, z, :], strips[1, y, z, :]
            right = jnp.where(low, first, second)
            left = pltpu.roll(jnp.where(low, second, first), 3 * STRIP, 1)
            pair[y, z, :] = jnp.where(right_first, right, left)
            after[y, z, :] = jnp.where(right_first, left, right)

    tiles(cells.shape[1], tile)


def split_depth_kernel(me, *rest):
    pieces, out = rest[:4], rest[4]
    for e in range(4):
        out[e] = pieces[e][:, slots(1 - me[2], out.shape[2]), :]


def gather_kernel(me, *rest):
    out = rest[10]
    for part in range(2):
        pieces, swapped = rest[5 * part : 5 * part + 4], rest[5 * part + 4]
        rows, depth = swapped.shape[1:3]
        y = slots(me[0] if part == 0 else 1 - me[0], rows)
        for e in range(4):
            yl, zh = chip(me, e)
            side = me[2] ^ yl
            out[zh, y, :, slots(2 * yl + side, LANES)] = pieces[e][:, slots(me[2], depth), :]
            out[zh, y, :, slots(2 * yl + 1 - side, LANES)] = swapped[e]


def pack_tile(me, z, cells, to_pair, to_next):
    groups = LANES // STRIP
    deep = len(cells) // groups
    lane_group = lax.broadcasted_iota(jnp.int32, (8, LANES), 1) // STRIP
    left_first = jnp.full((8, LANES), me[4], jnp.int32) == 1
    for y in range(deep):
        left = right = None
        for j in range(groups):
            cell = cells[deep * j + y]
            cell = pltpu.roll(cell, STRIP * j, 1) if j else cell
            left = cell if left is None else jnp.where(lane_group == j, cell, left)
            right = cell if right is None else jnp.where(lane_group == j - 1, cell, right)
        to_pair[y, z, :] = jnp.where(left_first, left, right)
        to_next[y, z, :] = jnp.where(left_first, right, left)


def tiles(depth, body):
    def one(t, _):
        body(pl.ds(pl.multiple_of(8 * t, 8), 8))
        return 0

    lax.fori_loop(0, depth // 8, one, 0)


def weights_kernel(me, rows, columns, axial, listed, theirs, *outs):
    live = outs[-1]
    tall, deep = live.shape[0] // 2, live.shape[1] // listed.shape[0] // BZ
    wide = listed.shape[1] // tall // deep
    for lists, half in ((listed, me[0]), (theirs, 1 - me[0])):
        for g in range(lists.shape[0]):
            bits = jnp.int32(0)
            for i in range(lists.shape[1]):
                number = lists[g, i]
                bits = bits | jnp.where(number < 0, 0, jnp.left_shift(jnp.int32(1), jnp.maximum(number, 0)))
            for t in range(tall):
                for b in range(deep):
                    number = (t * deep + b) * wide + 2 * me[0] + me[4]
                    z = (g * deep + b) * BZ
                    hit = jnp.right_shift(bits, number) & 1
                    live[half * tall + t, z : z + BZ, :] = jnp.full((BZ, LANES), hit, jnp.int32).astype(F32)
    channel = me[1]
    nx, nz = LANES, outs[0].shape[0] // 4
    radius, reach = columns.shape[1] // 2, axial.shape[1] // 2

    totals = {}
    for taps in (rows, columns, axial):
        total = taps[channel, 0]
        for k in range(1, taps.shape[1]):
            total = total + taps[channel, k]
        totals[id(taps)] = total

    def toeplitz(taps, offsets):
        total = jnp.zeros(offsets.shape, F32)
        for k in range(taps.shape[1]):
            total = jnp.where(offsets == k, taps[channel, k], total)
        return total / totals[id(taps)]

    for flip in (False, True):
        wz, wx, wh, wy = outs[4 * flip : 4 * flip + 4]

        def offsets(source, target, half):
            return (target - source if flip else source - target) + half

        def iota(dims, axis):
            return lax.broadcasted_iota(jnp.int32, dims, axis)

        dims = (nz, 2 * nz)
        high, low = halves(toeplitz(axial, offsets(iota(dims, 1) % nz, iota(dims, 0), reach)))
        zero = jnp.zeros(dims, BF16)
        wz[...] = jnp.concatenate(
            [
                jnp.concatenate([high, zero], 1),
                jnp.concatenate([low, zero], 1),
                jnp.concatenate([zero, high], 1),
                jnp.concatenate([zero, low], 1),
            ],
            0,
        )
        dims = (nx, nx)
        high, low = halves(toeplitz(columns, offsets(iota(dims, 0), iota(dims, 1), radius)))
        both = jnp.concatenate([high, low], 1)
        wx[...] = jnp.concatenate([both, both], 0)
        dims = (STRIP, 2 * nx)
        lanes = iota(dims, 1)
        edge = lanes % (2 * STRIP)
        target = jnp.where(edge < STRIP, nx - STRIP + edge, edge - STRIP)
        groups = nx // STRIP
        for k, first in ((0, me[4] == 0), (1, me[4] == 1)):
            source = iota(dims, 0) + jnp.where(first, nx, -STRIP)
            high, low = halves(toeplitz(columns, offsets(source, target, radius)))
            for g in range(groups):
                here = lanes // (2 * STRIP) == jnp.where(first, g, (g + 1) % groups)
                at = k * nx + STRIP * g
                both = [jnp.where(here, part.astype(F32), 0.0).astype(BF16) for part in (high, low)]
                wh[at : at + STRIP, :] = jnp.concatenate(both, 1)
        for i in range(rows.shape[1]):
            k = rows.shape[1] - 1 - i if flip else i
            wy[i] = jnp.full((8, LANES), rows[channel, k], F32) / totals[id(rows)]


def blur_z(weights, slabs):
    depth = slabs[0].shape[0]
    parts = [jnp.concatenate(halves(slab), 0) for slab in slabs]
    stacked = jnp.concatenate(
        [jnp.concatenate(parts[:2], 0), jnp.concatenate(parts[2:], 0)], 1
    )
    out = dot(weights, stacked)
    return [
        out[2 * a * depth : (2 * a + 1) * depth, b * LANES : (b + 1) * LANES]
        + out[(2 * a + 1) * depth : (2 * a + 2) * depth, b * LANES : (b + 1) * LANES]
        for b in range(2)
        for a in range(2)
    ]


def own_columns(cells, wz, wx, out):
    rows, depth = cells.shape[:2]
    count = 16
    for first in range(0, rows, count):
        slabs = []
        for y in range(first, first + count, 4):
            slabs += blur_z(wz[...], [cells[y + i] for i in range(4)])
        both = dot(jnp.concatenate(halves(jnp.concatenate(slabs, 0)), 1), wx[...])
        out[first : first + count] = (both[:, :LANES] + both[:, LANES:]).reshape(count, depth, LANES)


def near_columns(own, pair, after, wz, wh, out):
    deep, depth = pair.shape[:2]
    a = blur_z(wz[...], [pair[i] for i in range(deep)])
    b = blur_z(wz[...], [after[i] for i in range(deep)])
    high_a, low_a = halves(jnp.concatenate(a, 0))
    high_b, low_b = halves(jnp.concatenate(b, 0))
    strips = jnp.concatenate(
        [jnp.concatenate([high_a, high_b], 1), jnp.concatenate([low_a, low_b], 1)], 0
    )
    both = dot(strips, wh[...])
    count, wide = deep * depth, both.shape[1] // 2
    both = both[:, :wide] + both[:, wide:]
    both = both[:count] + both[count:]
    lane = lax.broadcasted_iota(jnp.int32, (count, LANES), 1)
    near = (lane < STRIP) | (lane >= LANES - STRIP)
    per = LANES // (2 * STRIP)
    for j in range(LANES // STRIP):
        add = both[:, j // per * LANES : (j // per + 1) * LANES]
        add = pltpu.roll(add, (LANES - STRIP - 2 * STRIP * (j % per)) % LANES, 1)
        add = jnp.where(near, add, 0.0).reshape(deep, depth, LANES)
        out[deep * j : deep * (j + 1)] = own[deep * j : deep * (j + 1)] + add


def own_kernel(cells, wz, wx, out):
    own_columns(cells, wz, wx, out)


def outer_kernel(me, own, pair, after, wz, wh, out, send_a, send_b):
    near_columns(own, pair, after, wz, wh, out)
    rows, count = out.shape[0], send_a.shape[0]
    even = me[3] == 0

    @pl.when(even)
    def _():
        send_a[...] = out[rows - count :]
        send_b[...] = out[:count]

    @pl.when(jnp.logical_not(even))
    def _():
        send_a[...] = out[:count]
        send_b[...] = out[rows - count :]


def ratio(observed, blurred, live):
    return jnp.where(live != 0, observed / blurred, 1.0)


def product(estimate, correction, live):
    return jnp.where(live != 0, estimate * correction, estimate)


def blur_rows(wy, quarter, depth, outer, inner, pre, take):
    rows = 4 * quarter
    radius = wy.shape[0] // 2

    def source(y):
        if y < quarter:
            return outer, y
        if y < 3 * quarter:
            return inner, y - quarter
        return outer, y - 2 * quarter

    def tile(z):
        taps = [wy[i] for i in range(wy.shape[0])]
        for first in range(0, rows, quarter):
            sums = [None if pre is None else pre[first + o, z, :] for o in range(quarter)]
            for y in range(max(0, first - radius), min(rows, first + quarter + radius)):
                ref, at = source(y)
                if ref is None:
                    continue
                cell = ref[at, z, :]
                for o in range(quarter):
                    i = y - (first + o) + radius
                    if 0 <= i < len(taps):
                        term = taps[i] * cell
                        sums[o] = term if sums[o] is None else sums[o] + term
            for o in range(quarter):
                take(first + o, z, jnp.zeros((8, LANES), F32) if sums[o] is None else sums[o])

    tiles(depth, tile)


def ahead_kernel(outer, wy, pre):
    def take(y, z, value):
        pre[y, z, :] = value

    blur_rows(wy, outer.shape[0] // 2, outer.shape[1], outer, None, None, take)


def inner_blur(me, cells, pair, after, outer, pre, wz, wx, wh, wy, part, inner, body):
    own_columns(cells, wz, wx, inner)
    near_columns(inner, pair, after, wz, wh, inner)
    quarter, depth = inner.shape[0] // 2, inner.shape[1]
    blurred = []

    def take(y, z, value):
        if quarter <= y < 3 * quarter:
            blurred.append(value)
        else:
            part[y if y < quarter else y - 2 * quarter, z, :] = value
        if y == 4 * quarter - 1:
            body(z, blurred)
            blurred.clear()

    blur_rows(wy, quarter, depth, outer, inner, pre, take)


def outer_blur(me, part, recv_a, recv_b, wy, halo, body):
    rows, depth = part.shape[:2]
    radius = wy.shape[0] // 2
    even = me[3] == 0
    halo[jnp.where(even, 1, 0)] = recv_a[...]
    halo[jnp.where(even, 0, 1)] = recv_b[...]

    def tile(z):
        taps = [wy[i] for i in range(wy.shape[0])]
        sums = [part[y, z, :] for y in range(rows)]
        for side in range(2):
            for h in range(radius):
                y = h - radius if side == 0 else rows + h
                cell = halo[side, h, z, :]
                for o in range(radius) if side == 0 else range(rows - radius, rows):
                    i = y - o + radius
                    if 0 <= i < len(taps):
                        sums[o] = sums[o] + taps[i] * cell
        body(z, sums)

    tiles(depth, tile)


def bricks_of(outer, y):
    return y // BY if outer and y < 16 else y // BY + (4 if outer else 2)


def update(me, outer, rule, base, live, out, strips):
    def body(z, blurred):
        cells = []
        for y in range(len(blurred)):
            cells.append(rule(base[y, z, :], blurred[y], live[bricks_of(outer, y), z, :]))
            out[y, z, :] = cells[y]
        if strips:
            pack_tile(me, z, cells, *strips)

    return body


def deal_out(me, cells, pieces):
    rows, depth = pieces[0].shape[:2]
    for e in range(4):
        yl, zh = chip(me, e)
        pieces[e][...] = cells[slots(yl, rows), slots(zh, depth), :]


def inner_kernel(first, rule, me, cells, pair, after, known, wz, wx, wh, wy, base, live, part, out, to_pair, to_next, inner):
    body = update(me, False, rule, base, live, out, (to_pair, to_next))
    outer, pre = (None, known) if first else (known, None)
    inner_blur(me, cells, pair, after, outer, pre, wz, wx, wh, wy, part, inner, body)


def last_inner_kernel(me, cells, pair, after, outer, wz, wx, wh, wy, base, live, part, *rest):
    pieces, inner, out = rest[:4], rest[4], rest[5]
    body = update(me, False, product, base, live, out, ())
    inner_blur(me, cells, pair, after, outer, None, wz, wx, wh, wy, part, inner, body)
    deal_out(me, out, pieces)


def final_kernel(rule, me, part, recv_a, recv_b, wy, base, live, out, to_pair, to_next, halo):
    outer_blur(me, part, recv_a, recv_b, wy, halo, update(me, True, rule, base, live, out, (to_pair, to_next)))


def last_final_kernel(me, part, recv_a, recv_b, wy, base, live, *rest):
    pieces, halo, out = rest[:4], rest[4], rest[5]
    outer_blur(me, part, recv_a, recv_b, wy, halo, update(me, True, product, base, live, out, ()))
    deal_out(me, out, pieces)


def call(kernel, out, ins, scratch=(), us=1, name=None, mib=6):
    many = isinstance(out, (tuple, list))
    return pl.pallas_call(
        kernel,
        out_shape=out,
        in_specs=ins,
        out_specs=[VMEM] * len(out) if many else VMEM,
        scratch_shapes=list(scratch),
        compiler_params=pltpu.CompilerParams(vmem_limit_bytes=mib * MIB),
        cost_estimate=pl.CostEstimate(flops=int(us * 1.0e9), bytes_accessed=0, transcendentals=0),
        name=name,
    )


def per_device(observed, psf_rows, psf_columns, psf_axial, live_list):
    yh = lax.axis_index("yh")
    yl, zh, zl = lax.axis_index("yl"), lax.axis_index("zh"), lax.axis_index("zl")
    side = zl ^ yl
    me = jnp.stack([yl, zh, zl, yh % 2, side]).astype(jnp.int32)
    channels, rows, depth, columns = observed.shape
    ny, nz = 2 * rows, 4 * depth
    radius = psf_rows.shape[1] // 2
    swaps = [(0, 1), (1, 0)]

    def trade(pieces):
        return [pieces[0]] + [
            lax.ppermute(pieces[e], ("yl", "zh"), [(i, i ^ e) for i in range(4)]) for e in range(1, 4)
        ]

    half = shape((ny // 2, nz, LANES))
    strip = shape((ny // 2 // (LANES // STRIP), nz, LANES))
    halo = shape((radius, nz, LANES))
    swapped = shape((4, rows // 2, depth, LANES))
    along = shape((rows // 2, 2 * depth, LANES))

    listed = live_list[0]
    theirs = lax.ppermute(listed, "yl", swaps)
    mine = shape((channels, 2, rows + 8, depth, LANES))
    kept, sent = call(deal_kernel, [mine] * 2, [SMEM, VMEM], us=0, name="deal")(me, observed)
    swapped_in = lax.ppermute(sent, "zl", swaps)
    tall = shape((rows // 2 + 4, 2 * depth, LANES))

    dealt = call(mix_kernel, [tall] * 8, [SMEM] + [VMEM] * 2, us=0, name="mix")(me, kept, swapped_in)
    dealt, theirs = lax.optimization_barrier((dealt, theirs))
    outer_pieces = trade(dealt[:4])
    inner_pieces = trade(dealt[4:])

    wide = [
        shape((4 * nz, 4 * nz), BF16),
        shape((2 * LANES, 2 * LANES), BF16),
        shape((2 * LANES, 4 * LANES), BF16),
        shape((psf_rows.shape[1], 8, LANES)),
    ]
    later, _ = lax.optimization_barrier((me, dealt))
    *weights, live = call(
        weights_kernel, wide * 2 + [shape((ny // BY, nz, LANES))], [SMEM] * 6, us=1, name="weights", mib=8
    )(later, psf_rows, psf_columns, psf_axial, listed, theirs)
    outer_pieces, weights, live = lax.optimization_barrier((outer_pieces, weights, live))

    def take(pieces):
        room = pltpu.VMEM((2,) + strip.shape, F32)
        return call(join_kernel, [half, strip, strip], [SMEM] + [VMEM] * 4, [room], us=0.3, name="join")(me, *pieces)

    high = lax.axis_size("yh")
    evens = [p for i in range(0, high - 1, 2) for p in ((i, i + 1), (i + 1, i))]
    odds = [p for i in range(1, high - 1, 2) for p in ((i, i + 1), (i + 1, i))]

    def exchange(to_pair, to_next):
        after = lax.ppermute(to_next, ("yl", "zl"), [(1, 3), (3, 1)])
        return lax.ppermute(to_pair, "zl", swaps), after

    def send_outer(cells, beside, w, near):
        wz, wx, wh, wy = w
        pair, after = beside
        cells, near = lax.optimization_barrier((cells, near))
        own = call(own_kernel, half, [VMEM] * 3, us=0.3, name="own", mib=8)(cells, wz, wx)
        outer, send_a, send_b = call(
            outer_kernel, [half, halo, halo], [SMEM] + [VMEM] * 5, us=0.3, name="outer", mib=8
        )(me, own, pair, after, wz, wh)
        return outer, lax.ppermute(send_a, "yh", evens), lax.ppermute(send_b, "yh", odds), near

    room, beyond = pltpu.VMEM(half.shape, F32), pltpu.VMEM((2,) + halo.shape, F32)
    taken = [take(outer_pieces), None]
    estimate = [taken[0][0], None]
    cells, strips = list(estimate), [taken[0][1:], None]
    for step in range(2 * ITERS):
        w = weights[:4] if step % 2 == 0 else weights[4:]
        near = exchange(*strips[1]) if step else ()
        beside = exchange(*strips[0]) if step else strips[0]
        outer, recv_a, recv_b, near = send_outer(cells[0], beside, w, near)
        if step == 0:
            whole = shape((ny, nz, LANES))
            outer = call(ahead_kernel, whole, [VMEM] * 2, us=0.3, name="ahead")(outer, w[3])
            inner_pieces, outer = lax.optimization_barrier((inner_pieces, outer))
            taken[1] = take(inner_pieces)
            estimate[1] = cells[1] = taken[1][0]
            near = taken[1][1:]
        base = [taken[0][0], taken[1][0]] if step % 2 == 0 else estimate
        ins = (me, cells[1], *near, outer, *w, base[1], live)
        if step == 2 * ITERS - 1:
            part, *pieces = call(
                last_inner_kernel, [half] + [along] * 4, [SMEM] + [VMEM] * 10, [room, room], us=3, name="last_inner", mib=16
            )(*ins)
            inner_out = trade(pieces)
            outer_out = trade(
                call(last_final_kernel, [along] * 4, [SMEM] + [VMEM] * 6, [beyond, room], us=2, name="last", mib=8)(
                    me, part, recv_a, recv_b, w[3], base[0], live
                )
            )
            continue
        rule = ratio if step % 2 == 0 else product
        part, inner, *inner_strips = call(
            functools.partial(inner_kernel, step == 0, rule), [half, half, strip, strip], [SMEM] + [VMEM] * 10, [room], us=3,
            name="inner", mib=16,
        )(*ins)
        outer, *outer_strips = call(
            functools.partial(final_kernel, rule), [half, strip, strip], [SMEM] + [VMEM] * 6, [beyond], us=2,
            name="final", mib=8,
        )(me, part, recv_a, recv_b, w[3], base[0], live)
        cells, strips = [outer, inner], [outer_strips, inner_strips]
        if step % 2 == 1:
            estimate = cells

    def back(pieces):
        sent = call(split_depth_kernel, swapped, [SMEM] + [VMEM] * 4, us=1, name="split_back")(me, *pieces)
        return (*pieces, lax.ppermute(sent, "zl", swaps))

    return call(gather_kernel, shape(observed.shape), [SMEM] + [VMEM] * 10, us=2, name="gather", mib=8)(
        me, *back(outer_out), *back(inner_out)
    )


def solution(mesh):
    fine = Mesh(
        mesh.devices.reshape(mesh.devices.shape[0] // 2, 2, 2, mesh.devices.shape[1] // 2),
        ("yh", "yl", "zh", "zl"),
    )
    spread = P(None, ("yh", "yl"), ("zh", "zl"), None)
    placed = (spread, P(), P(), P(), P(("yh", "yl"), None, None))
    return jax.shard_map(per_device, mesh=fine, in_specs=placed, out_specs=spread, check_vma=False)
```

```python
import functools

import jax
import jax.numpy as jnp
from jax import lax
from jax.experimental import pallas as pl
from jax.experimental.pallas import tpu as pltpu
from jax.sharding import Mesh, PartitionSpec as P

ITERS = 2
BY = 8
BZ = 8
LANES = 128
STRIP = 16
F32, BF16 = jnp.float32, jnp.bfloat16
VMEM = pl.BlockSpec(memory_space=pltpu.VMEM)
SMEM = pl.BlockSpec(memory_space=pltpu.SMEM)
MIB = 1024 * 1024


def shape(dims, dtype=F32):
    return jax.ShapeDtypeStruct(dims, dtype)


def halves(cells):
    high = cells.astype(BF16)
    return high, (cells - high.astype(F32)).astype(BF16)


def dot(a, b):
    return jnp.dot(a, b, preferred_element_type=F32)


def chip(me, e):
    return tuple(jnp.where((e >> s) & 1, 1 - b, b) for b, s in ((me[0], 1), (me[1], 0)))


def slots(start, size):
    return pl.ds(pl.multiple_of(start * size, size), size)


def deal_kernel(me, observed, kept, sent):
    channels, rows, depth, columns = observed.shape
    lane_group = lax.broadcasted_iota(jnp.int32, (8, LANES), 1) // STRIP
    upper = jnp.full((8, LANES), me[0], jnp.int32) == 1
    for c in range(channels):
        for q in range(columns // LANES):
            cells = observed[c, :, :, q * LANES : (q + 1) * LANES]
            strips = {}
            for part in range(2):
                for y in range(4):
                    for t in range(depth // 8):
                        z = slice(8 * t, 8 * t + 8)
                        total = jnp.zeros((8, LANES), F32)
                        for g in range(4):
                            row = 16 * part + 4 * g + y
                            if (q + 1) * LANES < columns:
                                cell = observed[c, row, z, (q + 1) * LANES : (q + 2) * LANES]
                                total = jnp.where(lane_group == g, pltpu.roll(cell, STRIP * g, 1) if g else cell, total)
                            if q:
                                cell = observed[c, row, z, (q - 1) * LANES : q * LANES]
                                cell = pltpu.roll(cell, STRIP * (g + 5), 1)
                                total = jnp.where(lane_group == g + 4, cell, total)
                        strips[part, y, t] = jnp.where(upper, pltpu.roll(total, LANES // 2, 1), total)

            def put(out):
                out[c, q // 2, :rows] = cells
                for (part, y, t), value in strips.items():
                    out[c, q // 2, rows + 4 * part + y, 8 * t : 8 * t + 8, :] = value

            own = me[2] == (q % 2) ^ (q // 2)

            @pl.when(own)
            def _():
                put(kept)

            @pl.when(jnp.logical_not(own))
            def _():
                put(sent)


def mix_kernel(me, kept, swapped, *outs):
    rows, depth = outs[0].shape[0] - 4, kept.shape[3]
    for part in range(2):
        half = me[0] if part == 0 else 1 - me[0]
        for e in range(4):
            yl, zh = chip(me, e)
            out = outs[4 * part + e]
            for z, cells in ((me[2], kept), (1 - me[2], swapped)):
                out[:rows, slots(z, depth), :] = cells[zh, yl, slots(half, rows)]
                out[rows:, slots(z, depth), :] = cells[zh, yl, pl.ds(2 * rows + 4 * half, 4)]


def join_kernel(me, *rest):
    pieces, cells, pair, after, strips = rest[:4], rest[4], rest[5], rest[6], rest[7]
    rows, depth = pieces[0].shape[0] - 4, pieces[0].shape[1]
    for e in range(4):
        yl, zh = chip(me, e)
        z = slots(zh, depth)
        cells[slots(yl, rows), z, :] = pieces[e][:rows]
        strips[yl, :, z, :] = pieces[e][rows:]
    low = lax.broadcasted_iota(jnp.int32, (8, LANES), 1) < LANES // 2
    right_first = jnp.full((8, LANES), me[4], jnp.int32) == 0

    def tile(z):
        for y in range(4):
            first, second = strips[0, y, z, :], strips[1, y, z, :]
            right = jnp.where(low, first, second)
            left = pltpu.roll(jnp.where(low, second, first), 3 * STRIP, 1)
            pair[y, z, :] = jnp.where(right_first, right, left)
            after[y, z, :] = jnp.where(right_first, left, right)

    tiles(cells.shape[1], tile)


def split_depth_kernel(me, *rest):
    pieces, out = rest[:4], rest[4]
    for e in range(4):
        out[e] = pieces[e][:, slots(1 - me[2], out.shape[2]), :]


def gather_kernel(me, *rest):
    out = rest[10]
    for part in range(2):
        pieces, swapped = rest[5 * part : 5 * part + 4], rest[5 * part + 4]
        rows, depth = swapped.shape[1:3]
        y = slots(me[0] if part == 0 else 1 - me[0], rows)
        for e in range(4):
            yl, zh = chip(me, e)
            side = me[2] ^ yl
            out[zh, y, :, slots(2 * yl + side, LANES)] = pieces[e][:, slots(me[2], depth), :]
            out[zh, y, :, slots(2 * yl + 1 - side, LANES)] = swapped[e]


def pack_tile(me, z, cells, to_pair, to_next):
    groups = LANES // STRIP
    deep = len(cells) // groups
    lane_group = lax.broadcasted_iota(jnp.int32, (8, LANES), 1) // STRIP
    left_first = jnp.full((8, LANES), me[4], jnp.int32) == 1
    for y in range(deep):
        left = right = None
        for j in range(groups):
            cell = cells[deep * j + y]
            cell = pltpu.roll(cell, STRIP * j, 1) if j else cell
            left = cell if left is None else jnp.where(lane_group == j, cell, left)
            right = cell if right is None else jnp.where(lane_group == j - 1, cell, right)
        to_pair[y, z, :] = jnp.where(left_first, left, right)
        to_next[y, z, :] = jnp.where(left_first, right, left)


def tiles(depth, body):
    def one(t, _):
        body(pl.ds(pl.multiple_of(8 * t, 8), 8))
        return 0

    lax.fori_loop(0, depth // 8, one, 0)


def weights_kernel(me, rows, columns, axial, listed, theirs, *outs):
    live = outs[-1]
    tall, deep = live.shape[0] // 2, live.shape[1] // listed.shape[0] // BZ
    wide = listed.shape[1] // tall // deep
    for lists, half in ((listed, me[0]), (theirs, 1 - me[0])):
        for g in range(lists.shape[0]):
            bits = jnp.int32(0)
            for i in range(lists.shape[1]):
                number = lists[g, i]
                bits = bits | jnp.where(number < 0, 0, jnp.left_shift(jnp.int32(1), jnp.maximum(number, 0)))
            for t in range(tall):
                for b in range(deep):
                    number = (t * deep + b) * wide + 2 * me[0] + me[4]
                    z = (g * deep + b) * BZ
                    hit = jnp.right_shift(bits, number) & 1
                    live[half * tall + t, z : z + BZ, :] = jnp.full((BZ, LANES), hit, jnp.int32).astype(F32)
    channel = me[1]
    nx, nz = LANES, outs[0].shape[0] // 4
    radius, reach = columns.shape[1] // 2, axial.shape[1] // 2

    totals = {}
    for taps in (rows, columns, axial):
        total = taps[channel, 0]
        for k in range(1, taps.shape[1]):
            total = total + taps[channel, k]
        totals[id(taps)] = total

    def toeplitz(taps, offsets):
        total = jnp.zeros(offsets.shape, F32)
        for k in range(taps.shape[1]):
            total = jnp.where(offsets == k, taps[channel, k], total)
        return total / totals[id(taps)]

    for flip in (False, True):
        wz, wx, wh, wy = outs[4 * flip : 4 * flip + 4]

        def offsets(source, target, half):
            return (target - source if flip else source - target) + half

        def iota(dims, axis):
            return lax.broadcasted_iota(jnp.int32, dims, axis)

        dims = (nz, 2 * nz)
        high, low = halves(toeplitz(axial, offsets(iota(dims, 1) % nz, iota(dims, 0), reach)))
        zero = jnp.zeros(dims, BF16)
        wz[...] = jnp.concatenate(
            [
                jnp.concatenate([high, zero], 1),
                jnp.concatenate([low, zero], 1),
                jnp.concatenate([zero, high], 1),
                jnp.concatenate([zero, low], 1),
            ],
            0,
        )
        dims = (nx, nx)
        high, low = halves(toeplitz(columns, offsets(iota(dims, 0), iota(dims, 1), radius)))
        both = jnp.concatenate([high, low], 1)
        wx[...] = jnp.concatenate([both, both], 0)
        dims = (STRIP, 2 * nx)
        lanes = iota(dims, 1)
        edge = lanes % (2 * STRIP)
        target = jnp.where(edge < STRIP, nx - STRIP + edge, edge - STRIP)
        groups = nx // STRIP
        for k, first in ((0, me[4] == 0), (1, me[4] == 1)):
            source = iota(dims, 0) + jnp.where(first, nx, -STRIP)
            high, low = halves(toeplitz(columns, offsets(source, target, radius)))
            for g in range(groups):
                here = lanes // (2 * STRIP) == jnp.where(first, g, (g + 1) % groups)
                at = k * nx + STRIP * g
                both = [jnp.where(here, part.astype(F32), 0.0).astype(BF16) for part in (high, low)]
                wh[at : at + STRIP, :] = jnp.concatenate(both, 1)
        for i in range(rows.shape[1]):
            k = rows.shape[1] - 1 - i if flip else i
            wy[i] = jnp.full((8, LANES), rows[channel, k], F32) / totals[id(rows)]


def blur_z(weights, slabs):
    depth = slabs[0].shape[0]
    parts = [jnp.concatenate(halves(slab), 0) for slab in slabs]
    stacked = jnp.concatenate(
        [jnp.concatenate(parts[:2], 0), jnp.concatenate(parts[2:], 0)], 1
    )
    out = dot(weights, stacked)
    return [
        out[2 * a * depth : (2 * a + 1) * depth, b * LANES : (b + 1) * LANES]
        + out[(2 * a + 1) * depth : (2 * a + 2) * depth, b * LANES : (b + 1) * LANES]
        for b in range(2)
        for a in range(2)
    ]


def own_columns(cells, wz, wx, out):
    rows, depth = cells.shape[:2]
    count = 16
    for first in range(0, rows, count):
        slabs = []
        for y in range(first, first + count, 4):
            slabs += blur_z(wz[...], [cells[y + i] for i in range(4)])
        both = dot(jnp.concatenate(halves(jnp.concatenate(slabs, 0)), 1), wx[...])
        out[first : first + count] = (both[:, :LANES] + both[:, LANES:]).reshape(count, depth, LANES)


def near_columns(outer, own, pair, after, wz, wh, out):
    if len(pair.shape) == 4:
        pair, after = pair.at[0 if outer else 1], after.at[0 if outer else 1]
    deep, depth = pair.shape[:2]
    a = blur_z(wz[...], [pair[i] for i in range(deep)])
    b = blur_z(wz[...], [after[i] for i in range(deep)])
    high_a, low_a = halves(jnp.concatenate(a, 0))
    high_b, low_b = halves(jnp.concatenate(b, 0))
    strips = jnp.concatenate(
        [jnp.concatenate([high_a, high_b], 1), jnp.concatenate([low_a, low_b], 1)], 0
    )
    both = dot(strips, wh[...])
    count, wide = deep * depth, both.shape[1] // 2
    both = both[:, :wide] + both[:, wide:]
    both = both[:count] + both[count:]
    lane = lax.broadcasted_iota(jnp.int32, (count, LANES), 1)
    near = (lane < STRIP) | (lane >= LANES - STRIP)
    per = LANES // (2 * STRIP)
    for j in range(LANES // STRIP):
        add = both[:, j // per * LANES : (j // per + 1) * LANES]
        add = pltpu.roll(add, (LANES - STRIP - 2 * STRIP * (j % per)) % LANES, 1)
        add = jnp.where(near, add, 0.0).reshape(deep, depth, LANES)
        out[deep * j : deep * (j + 1)] = own[deep * j : deep * (j + 1)] + add


def own_kernel(cells, wz, wx, out):
    own_columns(cells, wz, wx, out)


def outer_kernel(me, own, pair, after, wz, wh, out, send_a, send_b):
    near_columns(True, own, pair, after, wz, wh, out)
    rows, count = out.shape[0], send_a.shape[0]
    even = me[3] == 0

    @pl.when(even)
    def _():
        send_a[...] = out[rows - count :]
        send_b[...] = out[:count]

    @pl.when(jnp.logical_not(even))
    def _():
        send_a[...] = out[:count]
        send_b[...] = out[rows - count :]


def ratio(observed, blurred, live):
    return jnp.where(live != 0, observed / blurred, 1.0)


def product(estimate, correction, live):
    return jnp.where(live != 0, estimate * correction, estimate)


def blur_rows(wy, quarter, depth, outer, inner, pre, take):
    rows = 4 * quarter
    radius = wy.shape[0] // 2

    def source(y):
        if y < quarter:
            return outer, y
        if y < 3 * quarter:
            return inner, y - quarter
        return outer, y - 2 * quarter

    def tile(z):
        taps = [wy[i] for i in range(wy.shape[0])]
        pairs = [taps[i] + taps[i + 1] if i + 1 < len(taps) else taps[i] for i in range(0, len(taps), 2)]

        def cell(y):
            ref, at = source(y) if 0 <= y < rows else (None, 0)
            return None if ref is None else ref[at, z, :]

        def difference(p, q):
            if p is None:
                return None if q is None else -q
            return p if q is None else p - q

        def add(total, tap, value):
            if value is None:
                return total
            return tap * value if total is None else total + tap * value

        for first in range(0, rows, quarter):
            count = quarter // 2
            shared, even, odd = ([None] * count for _ in range(3))
            for r in range(first - radius + 1, first + quarter + radius + 1, 2):
                middle = cell(r)
                before, behind = difference(cell(r - 1), middle), difference(cell(r + 1), middle)
                for o in range(count):
                    i = r - (first + 2 * o) + radius - 1
                    if 0 <= i < len(taps):
                        shared[o] = add(shared[o], pairs[i // 2], middle)
                        even[o] = add(even[o], taps[i], before)
                        if i + 1 < len(taps):
                            odd[o] = add(odd[o], taps[i + 1], behind)
            for o in range(count):
                for k, part in enumerate((even[o], odd[o])):
                    y = first + 2 * o + k
                    values = [v for v in (None if pre is None else pre[y, z, :], shared[o], part) if v is not None]
                    take(y, z, functools.reduce(jnp.add, values) if values else jnp.zeros((8, LANES), F32))

    tiles(depth, tile)


def ahead_kernel(outer, wy, pre):
    def take(y, z, value):
        pre[y, z, :] = value

    blur_rows(wy, outer.shape[0] // 2, outer.shape[1], outer, None, None, take)


def inner_blur(me, cells, pair, after, outer, pre, wz, wx, wh, wy, part, inner, body):
    own_columns(cells, wz, wx, inner)
    near_columns(False, inner, pair, after, wz, wh, inner)
    quarter, depth = inner.shape[0] // 2, inner.shape[1]
    blurred = []

    def take(y, z, value):
        if quarter <= y < 3 * quarter:
            blurred.append(value)
        else:
            part[y if y < quarter else y - 2 * quarter, z, :] = value
        if y == 4 * quarter - 1:
            body(z, blurred)
            blurred.clear()

    blur_rows(wy, quarter, depth, outer, inner, pre, take)


def outer_blur(me, part, recv_a, recv_b, wy, halo, body):
    rows, depth = part.shape[:2]
    radius = wy.shape[0] // 2
    even = me[3] == 0
    halo[jnp.where(even, 1, 0)] = recv_a[...]
    halo[jnp.where(even, 0, 1)] = recv_b[...]

    def tile(z):
        taps = [wy[i] for i in range(wy.shape[0])]
        sums = [part[y, z, :] for y in range(rows)]
        for side in range(2):
            for h in range(radius):
                y = h - radius if side == 0 else rows + h
                cell = halo[side, h, z, :]
                for o in range(radius) if side == 0 else range(rows - radius, rows):
                    i = y - o + radius
                    if 0 <= i < len(taps):
                        sums[o] = sums[o] + taps[i] * cell
        body(z, sums)

    tiles(depth, tile)


def bricks_of(outer, y):
    return y // BY if outer and y < 16 else y // BY + (4 if outer else 2)


def update(me, outer, rule, base, live, out, strips):
    def body(z, blurred):
        cells = []
        for y in range(len(blurred)):
            cells.append(rule(base[y, z, :], blurred[y], live[bricks_of(outer, y), z, :]))
            out[y, z, :] = cells[y]
        if strips:
            pack_tile(me, z, cells, *strips)

    return body


def deal_out(me, cells, pieces):
    rows, depth = pieces[0].shape[:2]
    for e in range(4):
        yl, zh = chip(me, e)
        pieces[e][...] = cells[slots(yl, rows), slots(zh, depth), :]


def inner_kernel(first, rule, me, cells, pair, after, known, wz, wx, wh, wy, base, live, part, out, to_pair, to_next, inner):
    body = update(me, False, rule, base, live, out, (to_pair, to_next))
    outer, pre = (None, known) if first else (known, None)
    inner_blur(me, cells, pair, after, outer, pre, wz, wx, wh, wy, part, inner, body)


def last_inner_kernel(me, cells, pair, after, outer, wz, wx, wh, wy, base, live, part, *rest):
    pieces, inner, out = rest[:4], rest[4], rest[5]
    body = update(me, False, product, base, live, out, ())
    inner_blur(me, cells, pair, after, outer, None, wz, wx, wh, wy, part, inner, body)
    deal_out(me, out, pieces)


def final_kernel(rule, me, part, recv_a, recv_b, wy, base, live, out, to_pair, to_next, halo):
    outer_blur(me, part, recv_a, recv_b, wy, halo, update(me, True, rule, base, live, out, (to_pair, to_next)))


def first_final_kernel(me, part, recv_a, recv_b, wy, base, live, pair, after, out, to_pair, to_next, halo):
    to_pair[1], to_next[1] = pair[...], after[...]
    body = update(me, True, ratio, base, live, out, (to_pair.at[0], to_next.at[0]))
    outer_blur(me, part, recv_a, recv_b, wy, halo, body)


def last_final_kernel(me, part, recv_a, recv_b, wy, base, live, *rest):
    pieces, halo, out = rest[:4], rest[4], rest[5]
    outer_blur(me, part, recv_a, recv_b, wy, halo, update(me, True, product, base, live, out, ()))
    deal_out(me, out, pieces)


def call(kernel, out, ins, scratch=(), us=1, name=None, mib=6):
    many = isinstance(out, (tuple, list))
    return pl.pallas_call(
        kernel,
        out_shape=out,
        in_specs=ins,
        out_specs=[VMEM] * len(out) if many else VMEM,
        scratch_shapes=list(scratch),
        compiler_params=pltpu.CompilerParams(vmem_limit_bytes=mib * MIB),
        cost_estimate=pl.CostEstimate(flops=int(us * 1.0e9), bytes_accessed=0, transcendentals=0),
        name=name,
    )


def per_device(observed, psf_rows, psf_columns, psf_axial, live_list):
    yh = lax.axis_index("yh")
    yl, zh, zl = lax.axis_index("yl"), lax.axis_index("zh"), lax.axis_index("zl")
    side = zl ^ yl
    me = jnp.stack([yl, zh, zl, yh % 2, side]).astype(jnp.int32)
    channels, rows, depth, columns = observed.shape
    ny, nz = 2 * rows, 4 * depth
    radius = psf_rows.shape[1] // 2
    swaps = [(0, 1), (1, 0)]

    def trade(pieces):
        return [pieces[0]] + [
            lax.ppermute(pieces[e], ("yl", "zh"), [(i, i ^ e) for i in range(4)]) for e in range(1, 4)
        ]

    half = shape((ny // 2, nz, LANES))
    strip = shape((ny // 2 // (LANES // STRIP), nz, LANES))
    halo = shape((radius, nz, LANES))
    swapped = shape((4, rows // 2, depth, LANES))
    along = shape((rows // 2, 2 * depth, LANES))

    listed = live_list[0]
    theirs = lax.ppermute(listed, "yl", swaps)
    mine = shape((channels, 2, rows + 8, depth, LANES))
    kept, sent = call(deal_kernel, [mine] * 2, [SMEM, VMEM], us=0, name="deal")(me, observed)
    swapped_in = lax.ppermute(sent, "zl", swaps)
    tall = shape((rows // 2 + 4, 2 * depth, LANES))

    dealt = call(mix_kernel, [tall] * 8, [SMEM] + [VMEM] * 2, us=0, name="mix")(me, kept, swapped_in)
    dealt, theirs = lax.optimization_barrier((dealt, theirs))
    outer_pieces = trade(dealt[:4])
    inner_pieces = trade(dealt[4:])

    wide = [
        shape((4 * nz, 4 * nz), BF16),
        shape((2 * LANES, 2 * LANES), BF16),
        shape((2 * LANES, 4 * LANES), BF16),
        shape((psf_rows.shape[1], 8, LANES)),
    ]
    later, _ = lax.optimization_barrier((me, dealt))
    *weights, live = call(
        weights_kernel, wide * 2 + [shape((ny // BY, nz, LANES))], [SMEM] * 6, us=1, name="weights", mib=8
    )(later, psf_rows, psf_columns, psf_axial, listed, theirs)
    outer_pieces, weights, live = lax.optimization_barrier((outer_pieces, weights, live))

    def take(pieces):
        room = pltpu.VMEM((2,) + strip.shape, F32)
        return call(join_kernel, [half, strip, strip], [SMEM] + [VMEM] * 4, [room], us=0.3, name="join")(me, *pieces)

    high = lax.axis_size("yh")
    evens = [p for i in range(0, high - 1, 2) for p in ((i, i + 1), (i + 1, i))]
    odds = [p for i in range(1, high - 1, 2) for p in ((i, i + 1), (i + 1, i))]

    def exchange(to_pair, to_next):
        after = lax.ppermute(to_next, ("yl", "zl"), [(1, 3), (3, 1)])
        return lax.ppermute(to_pair, "zl", swaps), after

    def send_outer(cells, beside, w, near):
        wz, wx, wh, wy = w
        pair, after = beside
        cells, near = lax.optimization_barrier((cells, near))
        own = call(own_kernel, half, [VMEM] * 3, us=0.3, name="own", mib=8)(cells, wz, wx)
        outer, send_a, send_b = call(
            outer_kernel, [half, halo, halo], [SMEM] + [VMEM] * 5, us=0.3, name="outer", mib=8
        )(me, own, pair, after, wz, wh)
        return outer, lax.ppermute(send_a, "yh", evens), lax.ppermute(send_b, "yh", odds), near

    room, beyond = pltpu.VMEM(half.shape, F32), pltpu.VMEM((2,) + halo.shape, F32)
    taken = [take(outer_pieces), None]
    estimate = [taken[0][0], None]
    cells, strips = list(estimate), [taken[0][1:], None]
    for step in range(2 * ITERS):
        w = weights[:4] if step % 2 == 0 else weights[4:]
        near = exchange(*strips[1]) if step > 1 else ()
        beside = exchange(*strips[0]) if step else strips[0]
        outer, recv_a, recv_b, near = send_outer(cells[0], beside, w, near)
        if step == 1:
            near = beside
        if step == 0:
            whole = shape((ny, nz, LANES))
            outer = call(ahead_kernel, whole, [VMEM] * 2, us=0.3, name="ahead")(outer, w[3])
            inner_pieces, outer = lax.optimization_barrier((inner_pieces, outer))
            taken[1] = take(inner_pieces)
            estimate[1] = cells[1] = taken[1][0]
            near = taken[1][1:]
        base = [taken[0][0], taken[1][0]] if step % 2 == 0 else estimate
        ins = (me, cells[1], *near, outer, *w, base[1], live)
        if step == 2 * ITERS - 1:
            part, *pieces = call(
                last_inner_kernel, [half] + [along] * 4, [SMEM] + [VMEM] * 10, [room, room], us=3, name="last_inner", mib=16
            )(*ins)
            inner_out = trade(pieces)
            outer_out = trade(
                call(last_final_kernel, [along] * 4, [SMEM] + [VMEM] * 6, [beyond, room], us=2, name="last", mib=8)(
                    me, part, recv_a, recv_b, w[3], base[0], live
                )
            )
            continue
        rule = ratio if step % 2 == 0 else product
        part, inner, *inner_strips = call(
            functools.partial(inner_kernel, step == 0, rule), [half, half, strip, strip], [SMEM] + [VMEM] * 10, [room], us=3,
            name="inner", mib=16,
        )(*ins)
        ins = (me, part, recv_a, recv_b, w[3], base[0], live)
        if step == 0:
            outs, kernel, ins = [half] + [shape((2,) + strip.shape)] * 2, first_final_kernel, ins + tuple(inner_strips)
        else:
            outs, kernel = [half, strip, strip], functools.partial(final_kernel, rule)
        outer, *outer_strips = call(
            kernel, outs, [SMEM] + [VMEM] * (len(ins) - 1), [beyond], us=2, name="final", mib=8
        )(*ins)
        cells, strips = [outer, inner], [outer_strips, inner_strips]
        if step % 2 == 1:
            estimate = cells

    def back(pieces):
        sent = call(split_depth_kernel, swapped, [SMEM] + [VMEM] * 4, us=1, name="split_back")(me, *pieces)
        return (*pieces, lax.ppermute(sent, "zl", swaps))

    return call(gather_kernel, shape(observed.shape), [SMEM] + [VMEM] * 10, us=2, name="gather", mib=8)(
        me, *back(outer_out), *back(inner_out)
    )


def solution(mesh):
    fine = Mesh(
        mesh.devices.reshape(mesh.devices.shape[0] // 2, 2, 2, mesh.devices.shape[1] // 2),
        ("yh", "yl", "zh", "zl"),
    )
    spread = P(None, ("yh", "yl"), ("zh", "zl"), None)
    placed = (spread, P(), P(), P(), P(("yh", "yl"), None, None))
    return jax.shard_map(per_device, mesh=fine, in_specs=placed, out_specs=spread, check_vma=False)
```

```python
import functools

import jax
import jax.numpy as jnp
from jax import lax
from jax.experimental import pallas as pl
from jax.experimental.pallas import tpu as pltpu
from jax.sharding import Mesh, PartitionSpec as P

ITERS = 2
BY = 8
BZ = 8
LANES = 128
STRIP = 16
F32, BF16 = jnp.float32, jnp.bfloat16
VMEM = pl.BlockSpec(memory_space=pltpu.VMEM)
SMEM = pl.BlockSpec(memory_space=pltpu.SMEM)
MIB = 1024 * 1024


def shape(dims, dtype=F32):
    return jax.ShapeDtypeStruct(dims, dtype)


def halves(cells):
    high = cells.astype(BF16)
    return high, (cells - high.astype(F32)).astype(BF16)


def dot(a, b):
    return jnp.dot(a, b, preferred_element_type=F32)


def chip(me, e):
    return tuple(jnp.where((e >> s) & 1, 1 - b, b) for b, s in ((me[0], 1), (me[1], 0)))


def slots(start, size):
    return pl.ds(pl.multiple_of(start * size, size), size)


def deal_kernel(me, observed, kept, sent):
    channels, rows, depth, columns = observed.shape
    lane_group = lax.broadcasted_iota(jnp.int32, (8, LANES), 1) // STRIP
    upper = jnp.full((8, LANES), me[0], jnp.int32) == 1
    for c in range(channels):
        for q in range(columns // LANES):
            cells = observed[c, :, :, q * LANES : (q + 1) * LANES]
            strips = {}
            for part in range(2):
                for y in range(4):
                    for t in range(depth // 8):
                        z = slice(8 * t, 8 * t + 8)
                        total = jnp.zeros((8, LANES), F32)
                        for g in range(4):
                            row = 16 * part + 4 * g + y
                            if (q + 1) * LANES < columns:
                                cell = observed[c, row, z, (q + 1) * LANES : (q + 2) * LANES]
                                total = jnp.where(lane_group == g, pltpu.roll(cell, STRIP * g, 1) if g else cell, total)
                            if q:
                                cell = observed[c, row, z, (q - 1) * LANES : q * LANES]
                                cell = pltpu.roll(cell, STRIP * (g + 5), 1)
                                total = jnp.where(lane_group == g + 4, cell, total)
                        strips[part, y, t] = jnp.where(upper, pltpu.roll(total, LANES // 2, 1), total)

            def put(out):
                out[c, q // 2, :rows] = cells
                for (part, y, t), value in strips.items():
                    out[c, q // 2, rows + 4 * part + y, 8 * t : 8 * t + 8, :] = value

            own = me[2] == (q % 2) ^ (q // 2)

            @pl.when(own)
            def _():
                put(kept)

            @pl.when(jnp.logical_not(own))
            def _():
                put(sent)


def mix_kernel(me, kept, swapped, *outs):
    rows, depth = outs[0].shape[0] - 4, kept.shape[3]
    for part in range(2):
        half = me[0] if part == 0 else 1 - me[0]
        for e in range(4):
            yl, zh = chip(me, e)
            out = outs[4 * part + e]
            for z, cells in ((me[2], kept), (1 - me[2], swapped)):
                out[:rows, slots(z, depth), :] = cells[zh, yl, slots(half, rows)]
                out[rows:, slots(z, depth), :] = cells[zh, yl, pl.ds(2 * rows + 4 * half, 4)]


def join_kernel(me, *rest):
    pieces, cells, pair, after, strips = rest[:4], rest[4], rest[5], rest[6], rest[7]
    rows, depth = pieces[0].shape[0] - 4, pieces[0].shape[1]
    for e in range(4):
        yl, zh = chip(me, e)
        z = slots(zh, depth)
        cells[slots(yl, rows), z, :] = pieces[e][:rows]
        strips[yl, :, z, :] = pieces[e][rows:]
    low = lax.broadcasted_iota(jnp.int32, (8, LANES), 1) < LANES // 2
    right_first = jnp.full((8, LANES), me[4], jnp.int32) == 0

    def tile(z):
        for y in range(4):
            first, second = strips[0, y, z, :], strips[1, y, z, :]
            right = jnp.where(low, first, second)
            left = pltpu.roll(jnp.where(low, second, first), 3 * STRIP, 1)
            pair[y, z, :] = jnp.where(right_first, right, left)
            after[y, z, :] = jnp.where(right_first, left, right)

    tiles(cells.shape[1], tile)


def split_depth_kernel(me, *rest):
    pieces, out = rest[:4], rest[4]
    for e in range(4):
        out[e] = pieces[e][:, slots(1 - me[2], out.shape[2]), :]


def gather_kernel(me, *rest):
    out = rest[10]
    for part in range(2):
        pieces, swapped = rest[5 * part : 5 * part + 4], rest[5 * part + 4]
        rows, depth = swapped.shape[1:3]
        y = slots(me[0] if part == 0 else 1 - me[0], rows)
        for e in range(4):
            yl, zh = chip(me, e)
            side = me[2] ^ yl
            out[zh, y, :, slots(2 * yl + side, LANES)] = pieces[e][:, slots(me[2], depth), :]
            out[zh, y, :, slots(2 * yl + 1 - side, LANES)] = swapped[e]


def pack_tile(me, z, cells, to_pair, to_next):
    groups = LANES // STRIP
    deep = len(cells) // groups
    lane_group = lax.broadcasted_iota(jnp.int32, (8, LANES), 1) // STRIP
    left_first = jnp.full((8, LANES), me[4], jnp.int32) == 1
    for y in range(deep):
        left = right = None
        for j in range(groups):
            cell = cells[deep * j + y]
            cell = pltpu.roll(cell, STRIP * j, 1) if j else cell
            left = cell if left is None else jnp.where(lane_group == j, cell, left)
            right = cell if right is None else jnp.where(lane_group == j - 1, cell, right)
        to_pair[y, z, :] = jnp.where(left_first, left, right)
        to_next[y, z, :] = jnp.where(left_first, right, left)


def tiles(depth, body):
    def one(t, _):
        body(pl.ds(pl.multiple_of(8 * t, 8), 8))
        return 0

    lax.fori_loop(0, depth // 8, one, 0, unroll=4)


def weights_kernel(me, rows, columns, axial, listed, theirs, *outs):
    live = outs[-1]
    tall, deep = live.shape[0] // 2, live.shape[1] // listed.shape[0] // BZ
    wide = listed.shape[1] // tall // deep
    for lists, half in ((listed, me[0]), (theirs, 1 - me[0])):
        for g in range(lists.shape[0]):
            bits = jnp.int32(0)
            for i in range(lists.shape[1]):
                number = lists[g, i]
                bits = bits | jnp.where(number < 0, 0, jnp.left_shift(jnp.int32(1), jnp.maximum(number, 0)))
            for t in range(tall):
                for b in range(deep):
                    number = (t * deep + b) * wide + 2 * me[0] + me[4]
                    z = (g * deep + b) * BZ
                    hit = jnp.right_shift(bits, number) & 1
                    live[half * tall + t, z : z + BZ, :] = jnp.full((BZ, LANES), hit, jnp.int32).astype(F32)
    channel = me[1]
    nx, nz = LANES, outs[0].shape[0] // 4
    radius, reach = columns.shape[1] // 2, axial.shape[1] // 2

    totals = {}
    for taps in (rows, columns, axial):
        total = taps[channel, 0]
        for k in range(1, taps.shape[1]):
            total = total + taps[channel, k]
        totals[id(taps)] = total

    def toeplitz(taps, offsets):
        total = jnp.zeros(offsets.shape, F32)
        for k in range(taps.shape[1]):
            total = jnp.where(offsets == k, taps[channel, k], total)
        return total / totals[id(taps)]

    for flip in (False, True):
        wz, wx, wh, wy = outs[4 * flip : 4 * flip + 4]

        def offsets(source, target, half):
            return (target - source if flip else source - target) + half

        def iota(dims, axis):
            return lax.broadcasted_iota(jnp.int32, dims, axis)

        dims = (nz, 2 * nz)
        high, low = halves(toeplitz(axial, offsets(iota(dims, 1) % nz, iota(dims, 0), reach)))
        zero = jnp.zeros(dims, BF16)
        wz[...] = jnp.concatenate(
            [
                jnp.concatenate([high, zero], 1),
                jnp.concatenate([low, zero], 1),
                jnp.concatenate([zero, high], 1),
                jnp.concatenate([zero, low], 1),
            ],
            0,
        )
        dims = (nx, nx)
        high, low = halves(toeplitz(columns, offsets(iota(dims, 0), iota(dims, 1), radius)))
        both = jnp.concatenate([high, low], 1)
        wx[...] = jnp.concatenate([both, both], 0)
        dims = (STRIP, 2 * nx)
        lanes = iota(dims, 1)
        edge = lanes % (2 * STRIP)
        target = jnp.where(edge < STRIP, nx - STRIP + edge, edge - STRIP)
        groups = nx // STRIP
        for k, first in ((0, me[4] == 0), (1, me[4] == 1)):
            source = iota(dims, 0) + jnp.where(first, nx, -STRIP)
            high, low = halves(toeplitz(columns, offsets(source, target, radius)))
            for g in range(groups):
                here = lanes // (2 * STRIP) == jnp.where(first, g, (g + 1) % groups)
                at = k * nx + STRIP * g
                both = [jnp.where(here, part.astype(F32), 0.0).astype(BF16) for part in (high, low)]
                wh[at : at + STRIP, :] = jnp.concatenate(both, 1)
        for i in range(rows.shape[1]):
            k = rows.shape[1] - 1 - i if flip else i
            wy[i] = jnp.full((8, LANES), rows[channel, k], F32) / totals[id(rows)]


def blur_z(weights, slabs):
    depth = slabs[0].shape[0]
    parts = [jnp.concatenate(halves(slab), 0) for slab in slabs]
    stacked = jnp.concatenate(
        [jnp.concatenate(parts[:2], 0), jnp.concatenate(parts[2:], 0)], 1
    )
    out = dot(weights, stacked)
    return [
        out[2 * a * depth : (2 * a + 1) * depth, b * LANES : (b + 1) * LANES]
        + out[(2 * a + 1) * depth : (2 * a + 2) * depth, b * LANES : (b + 1) * LANES]
        for b in range(2)
        for a in range(2)
    ]


def own_columns(cells, wz, wx, out):
    rows, depth = cells.shape[:2]
    count = 16
    for first in range(0, rows, count):
        slabs = []
        for y in range(first, first + count, 4):
            slabs += blur_z(wz[...], [cells[y + i] for i in range(4)])
        both = dot(jnp.concatenate(halves(jnp.concatenate(slabs, 0)), 1), wx[...])
        out[first : first + count] = (both[:, :LANES] + both[:, LANES:]).reshape(count, depth, LANES)


def near_columns(outer, own, pair, after, wz, wh, out):
    if len(pair.shape) == 4:
        pair, after = pair.at[0 if outer else 1], after.at[0 if outer else 1]
    deep, depth = pair.shape[:2]
    a = blur_z(wz[...], [pair[i] for i in range(deep)])
    b = blur_z(wz[...], [after[i] for i in range(deep)])
    high_a, low_a = halves(jnp.concatenate(a, 0))
    high_b, low_b = halves(jnp.concatenate(b, 0))
    strips = jnp.concatenate(
        [jnp.concatenate([high_a, high_b], 1), jnp.concatenate([low_a, low_b], 1)], 0
    )
    both = dot(strips, wh[...])
    count, wide = deep * depth, both.shape[1] // 2
    both = both[:, :wide] + both[:, wide:]
    both = both[:count] + both[count:]
    lane = lax.broadcasted_iota(jnp.int32, (count, LANES), 1)
    near = (lane < STRIP) | (lane >= LANES - STRIP)
    per = LANES // (2 * STRIP)
    for j in range(LANES // STRIP):
        add = both[:, j // per * LANES : (j // per + 1) * LANES]
        add = pltpu.roll(add, (LANES - STRIP - 2 * STRIP * (j % per)) % LANES, 1)
        add = jnp.where(near, add, 0.0).reshape(deep, depth, LANES)
        out[deep * j : deep * (j + 1)] = own[deep * j : deep * (j + 1)] + add


def own_kernel(cells, wz, wx, out):
    own_columns(cells, wz, wx, out)


def outer_kernel(me, own, pair, after, wz, wh, out, send_a, send_b):
    near_columns(True, own, pair, after, wz, wh, out)
    rows, count = out.shape[0], send_a.shape[0]
    even = me[3] == 0

    @pl.when(even)
    def _():
        send_a[...] = out[rows - count :]
        send_b[...] = out[:count]

    @pl.when(jnp.logical_not(even))
    def _():
        send_a[...] = out[:count]
        send_b[...] = out[rows - count :]


def ratio(observed, blurred, live):
    return jnp.where(live != 0, observed / blurred, 1.0)


def product(estimate, correction, live):
    return jnp.where(live != 0, estimate * correction, estimate)


def blur_rows(wy, quarter, depth, outer, inner, pre, take):
    rows = 4 * quarter
    radius = wy.shape[0] // 2

    def source(y):
        if y < quarter:
            return outer, y
        if y < 3 * quarter:
            return inner, y - quarter
        return outer, y - 2 * quarter

    def tile(z):
        taps = [wy[i] for i in range(wy.shape[0])]
        pairs = [taps[i] + taps[i + 1] if i + 1 < len(taps) else taps[i] for i in range(0, len(taps), 2)]

        def cell(y):
            ref, at = source(y) if 0 <= y < rows else (None, 0)
            return None if ref is None else ref[at, z, :]

        def difference(p, q):
            if p is None:
                return None if q is None else -q
            return p if q is None else p - q

        def add(total, tap, value):
            if value is None:
                return total
            return tap * value if total is None else total + tap * value

        for first in range(0, rows, quarter):
            count = quarter // 2
            shared, even, odd = ([None] * count for _ in range(3))
            for r in range(first - radius + 1, first + quarter + radius + 1, 2):
                middle = cell(r)
                before, behind = difference(cell(r - 1), middle), difference(cell(r + 1), middle)
                for o in range(count):
                    i = r - (first + 2 * o) + radius - 1
                    if 0 <= i < len(taps):
                        shared[o] = add(shared[o], pairs[i // 2], middle)
                        even[o] = add(even[o], taps[i], before)
                        if i + 1 < len(taps):
                            odd[o] = add(odd[o], taps[i + 1], behind)
            for o in range(count):
                for k, part in enumerate((even[o], odd[o])):
                    y = first + 2 * o + k
                    values = [v for v in (None if pre is None else pre[y, z, :], shared[o], part) if v is not None]
                    take(y, z, functools.reduce(jnp.add, values) if values else jnp.zeros((8, LANES), F32))

    tiles(depth, tile)


def ahead_kernel(outer, wy, pre):
    def take(y, z, value):
        pre[y, z, :] = value

    blur_rows(wy, outer.shape[0] // 2, outer.shape[1], outer, None, None, take)


def inner_blur(me, cells, pair, after, outer, pre, wz, wx, wh, wy, part, inner, body):
    own_columns(cells, wz, wx, inner)
    near_columns(False, inner, pair, after, wz, wh, inner)
    quarter, depth = inner.shape[0] // 2, inner.shape[1]
    blurred = []

    def take(y, z, value):
        if quarter <= y < 3 * quarter:
            blurred.append(value)
        else:
            part[y if y < quarter else y - 2 * quarter, z, :] = value
        if y == 4 * quarter - 1:
            body(z, blurred)
            blurred.clear()

    blur_rows(wy, quarter, depth, outer, inner, pre, take)


def outer_blur(me, part, recv_a, recv_b, wy, halo, body):
    rows, depth = part.shape[:2]
    radius = wy.shape[0] // 2
    even = me[3] == 0
    halo[jnp.where(even, 1, 0)] = recv_a[...]
    halo[jnp.where(even, 0, 1)] = recv_b[...]

    def tile(z):
        taps = [wy[i] for i in range(wy.shape[0])]
        sums = [part[y, z, :] for y in range(rows)]
        for side in range(2):
            for h in range(radius):
                y = h - radius if side == 0 else rows + h
                cell = halo[side, h, z, :]
                for o in range(radius) if side == 0 else range(rows - radius, rows):
                    i = y - o + radius
                    if 0 <= i < len(taps):
                        sums[o] = sums[o] + taps[i] * cell
        body(z, sums)

    tiles(depth, tile)


def bricks_of(outer, y):
    return y // BY if outer and y < 16 else y // BY + (4 if outer else 2)


def update(me, outer, rule, base, live, out, strips):
    def body(z, blurred):
        cells = []
        for y in range(len(blurred)):
            cells.append(rule(base[y, z, :], blurred[y], live[bricks_of(outer, y), z, :]))
            out[y, z, :] = cells[y]
        if strips:
            pack_tile(me, z, cells, *strips)

    return body


def deal_out(me, cells, pieces):
    rows, depth = pieces[0].shape[:2]
    for e in range(4):
        yl, zh = chip(me, e)
        pieces[e][...] = cells[slots(yl, rows), slots(zh, depth), :]


def inner_kernel(first, rule, me, cells, pair, after, known, wz, wx, wh, wy, base, live, part, out, to_pair, to_next, inner):
    body = update(me, False, rule, base, live, out, (to_pair, to_next))
    outer, pre = (None, known) if first else (known, None)
    inner_blur(me, cells, pair, after, outer, pre, wz, wx, wh, wy, part, inner, body)


def last_inner_kernel(me, cells, pair, after, outer, wz, wx, wh, wy, base, live, part, *rest):
    pieces, inner, out = rest[:4], rest[4], rest[5]
    body = update(me, False, product, base, live, out, ())
    inner_blur(me, cells, pair, after, outer, None, wz, wx, wh, wy, part, inner, body)
    deal_out(me, out, pieces)


def final_kernel(rule, me, part, recv_a, recv_b, wy, base, live, out, to_pair, to_next, halo):
    outer_blur(me, part, recv_a, recv_b, wy, halo, update(me, True, rule, base, live, out, (to_pair, to_next)))


def first_final_kernel(me, part, recv_a, recv_b, wy, base, live, pair, after, out, to_pair, to_next, halo):
    to_pair[1], to_next[1] = pair[...], after[...]
    body = update(me, True, ratio, base, live, out, (to_pair.at[0], to_next.at[0]))
    outer_blur(me, part, recv_a, recv_b, wy, halo, body)


def last_final_kernel(me, part, recv_a, recv_b, wy, base, live, *rest):
    pieces, halo, out = rest[:4], rest[4], rest[5]
    outer_blur(me, part, recv_a, recv_b, wy, halo, update(me, True, product, base, live, out, ()))
    deal_out(me, out, pieces)


def call(kernel, out, ins, scratch=(), us=1, name=None, mib=6):
    many = isinstance(out, (tuple, list))
    return pl.pallas_call(
        kernel,
        out_shape=out,
        in_specs=ins,
        out_specs=[VMEM] * len(out) if many else VMEM,
        scratch_shapes=list(scratch),
        compiler_params=pltpu.CompilerParams(vmem_limit_bytes=mib * MIB),
        cost_estimate=pl.CostEstimate(flops=int(us * 1.0e9), bytes_accessed=0, transcendentals=0),
        name=name,
    )


def per_device(observed, psf_rows, psf_columns, psf_axial, live_list):
    yh = lax.axis_index("yh")
    yl, zh, zl = lax.axis_index("yl"), lax.axis_index("zh"), lax.axis_index("zl")
    side = zl ^ yl
    me = jnp.stack([yl, zh, zl, yh % 2, side]).astype(jnp.int32)
    channels, rows, depth, columns = observed.shape
    ny, nz = 2 * rows, 4 * depth
    radius = psf_rows.shape[1] // 2
    swaps = [(0, 1), (1, 0)]

    def trade(pieces):
        return [pieces[0]] + [
            lax.ppermute(pieces[e], ("yl", "zh"), [(i, i ^ e) for i in range(4)]) for e in range(1, 4)
        ]

    half = shape((ny // 2, nz, LANES))
    strip = shape((ny // 2 // (LANES // STRIP), nz, LANES))
    halo = shape((radius, nz, LANES))
    swapped = shape((4, rows // 2, depth, LANES))
    along = shape((rows // 2, 2 * depth, LANES))

    listed = live_list[0]
    theirs = lax.ppermute(listed, "yl", swaps)
    mine = shape((channels, 2, rows + 8, depth, LANES))
    kept, sent = call(deal_kernel, [mine] * 2, [SMEM, VMEM], us=0, name="deal")(me, observed)
    swapped_in = lax.ppermute(sent, "zl", swaps)
    tall = shape((rows // 2 + 4, 2 * depth, LANES))

    dealt = call(mix_kernel, [tall] * 8, [SMEM] + [VMEM] * 2, us=0, name="mix")(me, kept, swapped_in)
    dealt, theirs = lax.optimization_barrier((dealt, theirs))
    outer_pieces = trade(dealt[:4])
    inner_pieces = trade(dealt[4:])

    wide = [
        shape((4 * nz, 4 * nz), BF16),
        shape((2 * LANES, 2 * LANES), BF16),
        shape((2 * LANES, 4 * LANES), BF16),
        shape((psf_rows.shape[1], 8, LANES)),
    ]
    later, _ = lax.optimization_barrier((me, dealt))
    *weights, live = call(
        weights_kernel, wide * 2 + [shape((ny // BY, nz, LANES))], [SMEM] * 6, us=1, name="weights", mib=8
    )(later, psf_rows, psf_columns, psf_axial, listed, theirs)
    outer_pieces, weights, live = lax.optimization_barrier((outer_pieces, weights, live))

    def take(pieces):
        room = pltpu.VMEM((2,) + strip.shape, F32)
        return call(join_kernel, [half, strip, strip], [SMEM] + [VMEM] * 4, [room], us=0.3, name="join")(me, *pieces)

    high = lax.axis_size("yh")
    evens = [p for i in range(0, high - 1, 2) for p in ((i, i + 1), (i + 1, i))]
    odds = [p for i in range(1, high - 1, 2) for p in ((i, i + 1), (i + 1, i))]

    def exchange(to_pair, to_next):
        after = lax.ppermute(to_next, ("yl", "zl"), [(1, 3), (3, 1)])
        return lax.ppermute(to_pair, "zl", swaps), after

    def send_outer(cells, beside, w, near):
        wz, wx, wh, wy = w
        pair, after = beside
        cells, near = lax.optimization_barrier((cells, near))
        own = call(own_kernel, half, [VMEM] * 3, us=0.3, name="own", mib=8)(cells, wz, wx)
        outer, send_a, send_b = call(
            outer_kernel, [half, halo, halo], [SMEM] + [VMEM] * 5, us=0.3, name="outer", mib=8
        )(me, own, pair, after, wz, wh)
        return outer, lax.ppermute(send_a, "yh", evens), lax.ppermute(send_b, "yh", odds), near

    room, beyond = pltpu.VMEM(half.shape, F32), pltpu.VMEM((2,) + halo.shape, F32)
    taken = [take(outer_pieces), None]
    estimate = [taken[0][0], None]
    cells, strips = list(estimate), [taken[0][1:], None]
    for step in range(2 * ITERS):
        w = weights[:4] if step % 2 == 0 else weights[4:]
        near = exchange(*strips[1]) if step > 1 else ()
        beside = exchange(*strips[0]) if step else strips[0]
        outer, recv_a, recv_b, near = send_outer(cells[0], beside, w, near)
        if step == 1:
            near = beside
        if step == 0:
            whole = shape((ny, nz, LANES))
            outer = call(ahead_kernel, whole, [VMEM] * 2, us=0.3, name="ahead")(outer, w[3])
            inner_pieces, outer = lax.optimization_barrier((inner_pieces, outer))
            taken[1] = take(inner_pieces)
            estimate[1] = cells[1] = taken[1][0]
            near = taken[1][1:]
        base = [taken[0][0], taken[1][0]] if step % 2 == 0 else estimate
        ins = (me, cells[1], *near, outer, *w, base[1], live)
        if step == 2 * ITERS - 1:
            part, *pieces = call(
                last_inner_kernel, [half] + [along] * 4, [SMEM] + [VMEM] * 10, [room, room], us=3, name="last_inner", mib=16
            )(*ins)
            inner_out = trade(pieces)
            outer_out = trade(
                call(last_final_kernel, [along] * 4, [SMEM] + [VMEM] * 6, [beyond, room], us=2, name="last", mib=8)(
                    me, part, recv_a, recv_b, w[3], base[0], live
                )
            )
            continue
        rule = ratio if step % 2 == 0 else product
        part, inner, *inner_strips = call(
            functools.partial(inner_kernel, step == 0, rule), [half, half, strip, strip], [SMEM] + [VMEM] * 10, [room], us=3,
            name="inner", mib=16,
        )(*ins)
        ins = (me, part, recv_a, recv_b, w[3], base[0], live)
        if step == 0:
            outs, kernel, ins = [half] + [shape((2,) + strip.shape)] * 2, first_final_kernel, ins + tuple(inner_strips)
        else:
            outs, kernel = [half, strip, strip], functools.partial(final_kernel, rule)
        outer, *outer_strips = call(
            kernel, outs, [SMEM] + [VMEM] * (len(ins) - 1), [beyond], us=2, name="final", mib=8
        )(*ins)
        cells, strips = [outer, inner], [outer_strips, inner_strips]
        if step % 2 == 1:
            estimate = cells

    def back(pieces):
        sent = call(split_depth_kernel, swapped, [SMEM] + [VMEM] * 4, us=1, name="split_back")(me, *pieces)
        return (*pieces, lax.ppermute(sent, "zl", swaps))

    return call(gather_kernel, shape(observed.shape), [SMEM] + [VMEM] * 10, us=2, name="gather", mib=8)(
        me, *back(outer_out), *back(inner_out)
    )


def solution(mesh):
    fine = Mesh(
        mesh.devices.reshape(mesh.devices.shape[0] // 2, 2, 2, mesh.devices.shape[1] // 2),
        ("yh", "yl", "zh", "zl"),
    )
    spread = P(None, ("yh", "yl"), ("zh", "zl"), None)
    placed = (spread, P(), P(), P(), P(("yh", "yl"), None, None))
    return jax.shard_map(per_device, mesh=fine, in_specs=placed, out_specs=spread, check_vma=False)
```
